32 devices in a mesh: section: 2 (over core), dp: 16 (over z, y, x).
Axes of the slice: x: 2, y: 2, z: 4, core: 2. Of those that a mesh axis runs over, the one named last changes fastest.
Arguments:
- entering: bfloat16 [2, 2, 64, 4096], P(None, None, None, 'dp'), may hold values from -6 to 6
- cotangent: bfloat16 [2, 2, 64, 4096], P(None, None, None, 'dp'), may hold values from -6 to 6
- weights: bfloat16 [2, 4096, 4096], P('section', 'dp'), may hold values from -0.09375 to 0.09375
Outputs:
- acts_down: bfloat16 [2, 2, 64, 4096], P('section', None, None, 'dp')
- acts_up: bfloat16 [2, 2, 64, 4096], P('section', None, None, 'dp')
- grads_down: bfloat16 [2, 2, 64, 4096], P('section', None, None, 'dp')
- grads_up: bfloat16 [2, 2, 64, 4096], P('section', None, None, 'dp')
- weight_grad: float32 [2, 4096, 4096], P('section', 'dp')
The draws below stay inside these ranges and needn't reach their ends.
All inputs are finite; a program needn't handle non-finite values.
Results may differ from the reference program's by a relative error of at most 0.0052.
Values may be sent and summed in bfloat16 or wider, within the bound.
A program may use at most 64 MiB of HBM per device.

```python
import jax
import jax.numpy as jnp
from jax import lax

D = 4096
TOK_MB = 64
MICRO = 2
LAYERS = 2


def block_scale(key, shape, split, low, high):
    factor_of, own = 1.0, jax.random.fold_in(key, 6)
    for axis_at, parts in split:
        steps = jnp.exp(jax.random.uniform(jax.random.fold_in(own, axis_at), (parts,), jnp.float32, low / len(split), high / len(split)))
        factor_of = factor_of * jnp.repeat(steps, shape[axis_at] // parts).reshape([-1 if axis == axis_at else 1 for axis in range(len(shape))])
    return factor_of


def bell_draw(key, shape, scale, reach, split=(), kind=jnp.bfloat16):
    entries = scale * jax.random.normal(key, shape, jnp.float32)
    if split:
        entries = entries * block_scale(key, shape, split, -0.22, 0.18)
    return jnp.clip(entries, -reach, reach).astype(kind)


def setup_inputs(seed: int = 0) -> dict:
    splits = jax.random.split(jax.random.key(seed), 4)
    entering = bell_draw(splits[0], (2, MICRO, TOK_MB, D), 1.0, 6.0, ((3, 16),))
    cotangent = bell_draw(splits[1], (2, MICRO, TOK_MB, D), 1.0, 6.0, ((3, 16),))
    weights = bell_draw(splits[2], (LAYERS, D, D), D ** -0.5, 0.09375, ((0, 2), (1, 16)))
    return dict(entering=entering, cotangent=cotangent, weights=weights)


NORM_EPS = 1e-05

def layer_forward(inputs, weight):
    values = inputs.astype(jnp.float32)
    row_scale = lax.rsqrt(lax.optimization_barrier(jnp.mean(values * values, axis=1, keepdims=True)) + NORM_EPS)
    normed = (values * row_scale).astype(jnp.bfloat16)
    mixed_cols = jnp.dot(normed, weight, preferred_element_type=jnp.float32)
    return ((values + mixed_cols).astype(jnp.bfloat16), normed, row_scale)

def layer_backward(slopes, normed, row_scale, weight):
    normed_f = normed.astype(jnp.float32)
    back_sum = lax.dot_general(slopes, weight, (((1,), (1,)), ((), ())), preferred_element_type=jnp.float32)
    row_dot = lax.optimization_barrier(jnp.sum(back_sum * normed_f, axis=1, keepdims=True))
    inputs_grad = (slopes.astype(jnp.float32) + row_scale * (back_sum - normed_f * row_dot / D)).astype(jnp.bfloat16)
    weight_step = lax.dot_general(normed, slopes, (((0,), (0,)), ((), ())), preferred_element_type=jnp.float32)
    return (inputs_grad, weight_step)

def reference(entering, cotangent, weights):
    layer_grads = [jnp.zeros((D, D), jnp.float32) for layer_idx in range(LAYERS)]
    outputs_all = []
    grads_all = []
    for stream in range(2):
        stream_outs = []
        stream_grads = []
        for micro_idx in range(MICRO):
            hidden = entering[stream, micro_idx]
            saved = []
            layer_outs = []
            for layer_idx in range(LAYERS):
                hidden, normed, row_scale = layer_forward(hidden, weights[layer_idx])
                saved.append((normed, row_scale))
                layer_outs.append(hidden)
            slopes = cotangent[stream, micro_idx]
            layer_backs = [None] * LAYERS
            for layer_idx in reversed(range(LAYERS)):
                slopes, weight_step = layer_backward(slopes, saved[layer_idx][0], saved[layer_idx][1], weights[layer_idx])
                layer_grads[layer_idx] = layer_grads[layer_idx] + weight_step
                layer_backs[layer_idx] = slopes
            stream_outs.append(jnp.stack(layer_outs))
            stream_grads.append(jnp.stack(layer_backs))
        outs_stack = jnp.stack(stream_outs, axis=1)
        grads_stack = jnp.stack(stream_grads, axis=1)
        if stream == 1:
            outs_stack = outs_stack[::-1]
            grads_stack = grads_stack[::-1]
        outputs_all.append(outs_stack)
        grads_all.append(grads_stack)
    return (outputs_all[0], outputs_all[1], grads_all[0], grads_all[1], jnp.stack(layer_grads))
```

```python
import jax
import jax.numpy as jnp
from jax import lax
from jax.experimental import pallas as pl
from jax.experimental.pallas import tpu as pltpu
from jax.sharding import PartitionSpec as P

NORM_EPS = 1e-05


def for_sending(value):

    def short(part):
        return part.astype(jnp.bfloat16) if part.dtype == jnp.float32 else part

    return jax.tree.map(short, value)


def from_behind(value, axis, steps):
    count = lax.axis_size(axis)
    first, last = (max(0, -steps), min(count, count - steps))
    return lax.ppermute(value, axis, [(source, source + steps) for source in range(first, last)])


def swapped_2(block, axis, apart):
    count = lax.axis_size(axis)
    route = []
    for low in range(count):
        high = low | 1 << apart
        if high != low and high < count:
            route += [(low, high), (high, low)]
    return lax.ppermute(block, axis, route)


def pass_along(payload, ahead):
    if ahead:
        return jax.tree.map(
            lambda part, own: part.astype(own.dtype),
            from_behind(for_sending(payload), "section", 1),
            payload,
        )
    return jax.tree.map(
        lambda part, own: part.astype(own.dtype),
        from_behind(for_sending(payload), "section", -1),
        payload,
    )


def send_pair(down_part, up_part, down_ahead):
    return jnp.stack([pass_along(down_part, down_ahead), pass_along(up_part, not down_ahead)])


def section_bits():
    return lax.axis_size("section").bit_length() - 1


def mirror_weights(payload):
    for bit_idx in range(section_bits()):
        payload = swapped_2(payload, "section", bit_idx)
    return payload


def mirror_grads(payload):
    for bit_idx in range(section_bits()):
        payload = swapped_2(payload.astype(jnp.bfloat16), "section", bit_idx).astype(payload.dtype)
    return payload


def row_totals(first_part, second_part):
    return lax.psum((first_part, second_part), "dp")


def place_slot(store, stream, slot_idx, payload, is_live):
    previous = lax.dynamic_index_in_dim(store[stream], slot_idx, 0, keepdims=False)
    kept = jnp.where(is_live, payload.astype(store.dtype), previous)
    zero_idx = jnp.zeros((), jnp.int32)
    starts = (jnp.int32(stream), slot_idx) + (zero_idx,) * (store.ndim - 2)
    return lax.dynamic_update_slice(store, kept[None, None], starts)


def forward_cols(full_rows, input_cols, weight_cols):
    values = full_rows.astype(jnp.float32)
    row_scale = lax.rsqrt(jnp.mean(values * values, axis=1, keepdims=True) + NORM_EPS)
    normed = (values * row_scale).astype(jnp.bfloat16)
    mixed_cols = jnp.dot(normed, weight_cols, preferred_element_type=jnp.float32)
    output_cols = (input_cols.astype(jnp.float32) + mixed_cols).astype(jnp.bfloat16)
    return (output_cols, normed, mixed_cols, row_scale[:, 0])


def body(entering, cotangent, weights):
    section_count = lax.axis_size("section")
    last_section = section_count - 1
    section_idx = lax.axis_index("section")
    group_count = lax.axis_size("dp")
    local_cols = weights.shape[1]
    model_width = weights.shape[2]
    col_start = lax.axis_index("dp") * local_cols
    micro_count = entering.shape[1]
    tok_rows = entering.shape[2]
    tick_count = micro_count + section_count - 1
    own_rows = weights[0]
    held_rows = jnp.stack([own_rows, mirror_weights(own_rows)])
    up_delay = last_section - section_idx
    held_count = held_rows.shape[0]
    split_rows = held_rows.reshape(held_count, local_cols, group_count, local_cols)
    swapped = lax.all_to_all(split_rows, "dp", split_axis=2, concat_axis=1, tiled=True)
    held_cols = swapped.reshape(held_count, model_width, local_cols)
    held_last = held_count - 1
    fwd_delays = (section_idx, up_delay)
    back_delays = (last_section - section_idx, last_section - up_delay)

    def slot_of(tick_idx, delay_now):
        micro_idx = tick_idx - delay_now
        slot_idx = jnp.clip(micro_idx, 0, micro_count - 1)
        is_live = (micro_idx >= 0) & (micro_idx < micro_count)
        return (slot_idx, is_live)

    def forward_tick(tick_idx, state_now):
        inbox, normed_store, mixed_store, scale_store, act_store = state_now
        inputs_now = []
        slots_now = []
        for stream in range(2):
            slot_idx, is_live = slot_of(tick_idx, fwd_delays[stream])
            fresh = lax.dynamic_index_in_dim(entering[stream], slot_idx, 0, keepdims=False)
            inputs_now.append(jnp.where(fwd_delays[stream] == 0, fresh, inbox[stream]))
            slots_now.append((slot_idx, is_live))
        full_down, full_up = (
            lax.all_gather(for_sending(inputs_now[0]), "dp", axis=1, tiled=True),
            lax.all_gather(for_sending(inputs_now[1]), "dp", axis=1, tiled=True),
        )
        outputs_now = []
        for stream, full_rows in enumerate((full_down, full_up)):
            output_cols, normed, mixed_cols, row_scale = forward_cols(
                full_rows, inputs_now[stream], held_cols[stream * held_last]
            )
            slot_idx, is_live = slots_now[stream]
            normed_store = place_slot(normed_store, stream, slot_idx, normed, is_live)
            mixed_store = place_slot(mixed_store, stream, slot_idx, mixed_cols, is_live)
            scale_store = place_slot(scale_store, stream, slot_idx, row_scale, is_live)
            act_store = place_slot(act_store, stream, slot_idx, output_cols, is_live)
            outputs_now.append(output_cols)
        inbox = send_pair(outputs_now[0], outputs_now[1], True)
        return (inbox, normed_store, mixed_store, scale_store, act_store)

    start_fwd = (
        jnp.zeros((2, tok_rows, local_cols), jnp.bfloat16),
        jnp.zeros((2, micro_count, tok_rows, model_width), jnp.bfloat16),
        jnp.zeros((2, micro_count, tok_rows, local_cols), jnp.float32),
        jnp.zeros((2, micro_count, tok_rows), jnp.float32),
        jnp.zeros((2, micro_count, tok_rows, local_cols), jnp.bfloat16),
    )
    ended_fwd = lax.fori_loop(0, tick_count, forward_tick, start_fwd)
    normed_store, mixed_store, scale_store, act_store = (
        ended_fwd[1],
        ended_fwd[2],
        ended_fwd[3],
        ended_fwd[4],
    )

    def backward_tick(tick_idx, state_now):
        inbox, grad_store, weight_acc = state_now
        slopes_now = []
        picks = []
        for stream in range(2):
            slot_idx, is_live = slot_of(tick_idx, back_delays[stream])
            fresh = lax.dynamic_index_in_dim(cotangent[stream], slot_idx, 0, keepdims=False)
            slopes_now.append(jnp.where(back_delays[stream] == 0, fresh, inbox[stream]))
            normed = lax.dynamic_index_in_dim(normed_store[stream], slot_idx, 0, keepdims=False)
            mixed_cols = lax.dynamic_index_in_dim(mixed_store[stream], slot_idx, 0, keepdims=False)
            row_scale = lax.dynamic_index_in_dim(scale_store[stream], slot_idx, 0, keepdims=False)
            picks.append((slot_idx, is_live, normed, mixed_cols, row_scale))
        slope_down, slope_up = (
            lax.all_gather(for_sending(slopes_now[0]), "dp", axis=1, tiled=True),
            lax.all_gather(for_sending(slopes_now[1]), "dp", axis=1, tiled=True),
        )
        slope_fulls = (slope_down, slope_up)
        back_sums = []
        normed_locals = []
        for stream in range(2):
            back_sums.append(
                lax.dot_general(
                    slope_fulls[stream],
                    held_rows[stream * held_last],
                    (((1,), (1,)), ((), ())),
                    preferred_element_type=jnp.float32,
                )
            )
            normed_locals.append(
                lax.dynamic_slice_in_dim(picks[stream][2], col_start, local_cols, 1)
            )
        row_sums = row_totals(
            jnp.sum(back_sums[0] * normed_locals[0].astype(jnp.float32), axis=1),
            jnp.sum(back_sums[1] * normed_locals[1].astype(jnp.float32), axis=1),
        )
        grads_now = []
        for stream in range(2):
            slot_idx, is_live, normed, mixed_cols, row_scale = picks[stream]
            row_dot = row_sums[stream][:, None]
            normed_part = normed_locals[stream].astype(jnp.float32)
            grad_cols = (
                slopes_now[stream].astype(jnp.float32)
                + row_scale[:, None] * (back_sums[stream] - normed_part * row_dot / model_width)
            ).astype(jnp.bfloat16)
            weight_step = lax.dot_general(
                normed_locals[stream],
                slope_fulls[stream],
                (((0,), (0,)), ((), ())),
                preferred_element_type=jnp.float32,
            )
            weight_acc = weight_acc.at[stream].add(weight_step * is_live.astype(jnp.float32))
            grad_store = place_slot(grad_store, stream, slot_idx, grad_cols, is_live)
            grads_now.append(grad_cols)
        inbox = send_pair(grads_now[0], grads_now[1], False)
        return (inbox, grad_store, weight_acc)

    start_back = (
        jnp.zeros((2, tok_rows, local_cols), jnp.bfloat16),
        jnp.zeros((2, micro_count, tok_rows, local_cols), jnp.bfloat16),
        jnp.zeros((2, local_cols, model_width), jnp.float32),
    )
    ended_back = lax.fori_loop(0, tick_count, backward_tick, start_back)
    grad_store, weight_acc = (ended_back[1], ended_back[2])
    total_grad = weight_acc[0] + mirror_grads(weight_acc[1])
    acts_up = act_store[1]
    grads_up = grad_store[1]
    return (
        act_store[0][None],
        acts_up[None],
        grad_store[0][None],
        grads_up[None],
        total_grad[None],
    )


MESH = pl.DeviceIdType.MESH
F32 = jnp.float32
BF16 = jnp.bfloat16
Z_ORDER = (1, 3, 2, 0)


def row_sums(values):
    ones = jnp.ones((8, values.shape[1]), F32)
    return lax.dot_general(
        ones,
        values,
        (((1,), (1,)), ((), ())),
        precision=lax.Precision.HIGHEST,
        preferred_element_type=F32,
    )


def window_kernel(
    h0, cot, w_hbm, ad, au, gd, gu, wg_hbm,
    w, gf, part, a1, b1, a2, b2, sa, sb, tz, zra, zrb, stats, back, hid, nrm, nrm_t, own, wg,
    w_sem, wg_sem, st_s, st_r, ag_s, ag_r, own_s, rs_s, rs_r, z_s, za_r, zb_r, ex_s, ex_r,
):
    tok, cols = h0.shape
    half = tok // 2
    low, high = pl.ds(0, half), pl.ds(half, half)
    width = cols * 16
    sec = lax.axis_index("section")
    dp = lax.axis_index("dp")
    z, y, x = dp // 4, (dp // 2) % 2, dp % 2
    px, py = dp + 1 - 2 * x, dp + 2 - 4 * y

    def zp(dz):
        return ((z + dz) % 4) * 4 + y * 2 + x

    def block_cols(dz, ry, rx):
        yy = 1 - y if ry else y
        xx = 1 - x if rx else x
        return pl.ds(pl.multiple_of((((z + dz) % 4) * 4 + yy * 2 + xx) * cols, cols), cols)

    def send(src, dst, s_sem, r_sem, section, chip):
        copy = pltpu.make_async_remote_copy(
            src_ref=src, dst_ref=dst, send_sem=s_sem, recv_sem=r_sem,
            device_id=(section, chip), device_id_type=MESH,
        )
        copy.start()
        return copy

    def arrived(dst, r_sem):
        pltpu.make_async_remote_copy(
            src_ref=dst, dst_ref=dst, send_sem=r_sem, recv_sem=r_sem,
            device_id=(sec, dp), device_id_type=MESH,
        ).wait_recv()

    load_w = pltpu.make_async_copy(w_hbm.at[0], w, w_sem)
    load_w.start()

    barrier = pltpu.get_barrier_semaphore()
    for step in range(1, 16):
        pl.semaphore_signal(barrier, inc=1, device_id=(sec, (dp + step) % 16), device_id_type=MESH)
    for chip in (dp, px, py, zp(1), zp(2), zp(3)):
        pl.semaphore_signal(barrier, inc=1, device_id=(1 - sec, chip), device_id_type=MESH)
    pl.semaphore_wait(barrier, 21)

    def stat_send(k, value):
        stats[k, dp] = value
        copies = []
        for step in range(1, 16):
            copies.append(send(
                stats.at[k, dp], stats.at[k, dp], st_s.at[k, step], st_r.at[k, step],
                sec, (dp + step) % 16,
            ))
        return copies

    def stat_total(k):
        for step in range(1, 16):
            arrived(stats.at[k, (dp + 16 - step) % 16], st_r.at[k, step])
        total = jnp.sum(stats[k], axis=0)
        return jnp.transpose(total)

    def gather_own(src, section, include_self):
        copies = []
        for dz in (1, 2, 3):
            copies.append(send(src, gf.at[4 - dz, 0, 0], own_s.at[dz], ag_r.at[4 - dz, 0], section, zp(dz)))
        copies.append(send(src, gf.at[0, 0, 1], own_s.at[4], ag_r.at[0, 1], section, px))
        copies.append(send(src, gf.at[0, 1, 0], own_s.at[5], ag_r.at[0, 2], section, py))
        if include_self:
            copies.append(send(src, gf.at[0, 0, 0], own_s.at[0], ag_r.at[0, 0], section, dp))
        return copies

    def gather_rest(use, own_arrives):
        copies = []
        for dz in (1, 3, 2):
            arrived(gf.at[dz, 0, 0], ag_r.at[dz, 0])
            copies.append(send(gf.at[dz, 0, 0], gf.at[dz, 0, 1], ag_s.at[dz, 0], ag_r.at[dz, 1], sec, px))
            copies.append(send(gf.at[dz, 0, 0], gf.at[dz, 1, 0], ag_s.at[dz, 1], ag_r.at[dz, 2], sec, py))
            if dz == 1:
                if own_arrives:
                    arrived(gf.at[0, 0, 0], ag_r.at[0, 0])
                use(0, 0, 0)
            use(dz, 0, 0)
        for dz in (0, 1, 3, 2):
            arrived(gf.at[dz, 0, 1], ag_r.at[dz, 1])
            copies.append(send(
                gf.at[dz, 0, 1, low], gf.at[dz, 1, 1, low], ag_s.at[dz, 2], ag_r.at[dz, 3], sec, py))
            arrived(gf.at[dz, 1, 0], ag_r.at[dz, 2])
            copies.append(send(
                gf.at[dz, 1, 0, high], gf.at[dz, 1, 1, high], ag_s.at[dz, 3], ag_r.at[dz, 4], sec, px))
            use(dz, 0, 1)
            use(dz, 1, 0)
        for dz in (0, 1, 3, 2):
            arrived(gf.at[dz, 1, 1, low], ag_r.at[dz, 3])
            arrived(gf.at[dz, 1, 1, high], ag_r.at[dz, 4])
            use(dz, 1, 1)
        return copies

    def scatter_first(rows):
        copies = []
        for dz in Z_ORDER:
            for ry, rx in ((0, 1), (1, 1), (1, 0), (0, 0)):
                part[dz, ry, rx] = jnp.dot(
                    rows[...], w[:, block_cols(dz, ry, rx)], preferred_element_type=F32
                ).astype(BF16)
                if (ry, rx) == (1, 1):
                    copies.append(send(
                        part.at[dz, pl.ds(0, 2), 1, low], a1.at[dz], rs_s.at[dz, 0], rs_r.at[dz, 0], sec, px))
                if (ry, rx) == (1, 0):
                    copies.append(send(
                        part.at[dz, 1, pl.ds(0, 2), high], b1.at[dz], rs_s.at[dz, 1], rs_r.at[dz, 1], sec, py))
        return copies

    def scatter_second():
        copies = []
        for dz in Z_ORDER:
            arrived(a1.at[dz], rs_r.at[dz, 0])
            sa[dz] = (part[dz, 1, 0, low].astype(F32) + a1[dz, 1].astype(F32)).astype(BF16)
            copies.append(send(sa.at[dz], a2.at[dz], rs_s.at[dz, 2], rs_r.at[dz, 2], sec, py))
            arrived(b1.at[dz], rs_r.at[dz, 1])
            sb[dz] = (part[dz, 0, 1, high].astype(F32) + b1[dz, 1].astype(F32)).astype(BF16)
            copies.append(send(sb.at[dz], b2.at[dz], rs_s.at[dz, 3], rs_r.at[dz, 3], sec, px))
        return copies

    def scatter_third(landing, r_sems, self_too):
        copies = []
        for dz in Z_ORDER:
            arrived(a2.at[dz], rs_r.at[dz, 2])
            tz[dz, low] = (
                part[dz, 0, 0, low].astype(F32) + a1[dz, 0].astype(F32) + a2[dz].astype(F32)
            ).astype(BF16)
            arrived(b2.at[dz], rs_r.at[dz, 3])
            tz[dz, high] = (
                part[dz, 0, 0, high].astype(F32) + b1[dz, 0].astype(F32) + b2[dz].astype(F32)
            ).astype(BF16)
            if dz:
                copies.append(send(tz.at[dz], landing.at[4 - dz], z_s.at[dz], r_sems.at[4 - dz], 1, zp(dz)))
            elif self_too:
                copies.append(send(tz.at[0], landing.at[0], z_s.at[0], r_sems.at[0], 1, dp))
        return copies

    def back_step(dz, ry, rx):
        return lax.dot_general(
            gf[dz, ry, rx], w[:, block_cols(dz, ry, rx)], (((1,), (1,)), ((), ())),
            preferred_element_type=F32,
        )

    def weight_step(dz, ry, rx):
        spot = block_cols(dz, ry, rx)
        wg[dz * 4 + ry * 2 + rx] = jnp.dot(nrm_t[...], gf[dz, ry, rx], preferred_element_type=F32)
        copy = pltpu.make_async_copy(
            wg.at[dz * 4 + ry * 2 + rx], wg_hbm.at[:, spot], wg_sem.at[dz * 4 + ry * 2 + rx])
        copy.start()
        return copy

    def scale_of(totals):
        return lax.rsqrt(totals[:, 0:1] / width + NORM_EPS)

    def set_normed(values, scale):
        normed = values.astype(F32) * scale
        nrm[...] = normed.astype(BF16)
        nrm_t[...] = jnp.transpose(normed).astype(BF16)

    entered = h0[...].astype(F32)

    @pl.when(sec == 0)
    def _():
        copies = stat_send(0, row_sums(entered * entered))
        load_w.wait()
        copies += scatter_first(h0)
        copies += scatter_second()
        copies += scatter_third(zra, za_r, True)
        scale = scale_of(stat_total(0))
        set_normed(h0[...], scale)
        back[...] = jnp.zeros_like(back)
        writes = []

        def use(dz, ry, rx):
            back[...] += back_step(dz, ry, rx)
            writes.append(weight_step(dz, ry, rx))

        copies += gather_rest(use, True)
        normed = nrm[...].astype(F32)
        copies += stat_send(2, row_sums(back[...] * normed))
        gu[...] = gf[0, 0, 0, high]
        arrived(ad, ex_r.at[0])
        dot = stat_total(2)[:, 0:1]
        own[...] = (
            gf[0, 0, 0].astype(F32) + scale * (back[...] - normed * dot / width)
        ).astype(BF16)
        copies.append(send(own.at[high], gu, ex_s.at[0], ex_r.at[1], 1, dp))
        gd[...] = own[low]
        arrived(au, ex_r.at[2])
        for copy in writes:
            copy.wait()
        for copy in copies:
            copy.wait_send()

    @pl.when(sec == 1)
    def _():
        copies = stat_send(0, row_sums(entered * entered))
        copies += gather_own(cot, 1, False)
        gf[0, 0, 0] = cot[...]
        back[...] = jnp.zeros_like(back)
        load_w.wait()

        def use(dz, ry, rx):
            back[...] += back_step(dz, ry, rx)

        copies += gather_rest(use, False)
        for copy in copies:
            copy.wait_send()
        scale = scale_of(stat_total(0))
        for dz in (0, 1, 3, 2):
            arrived(zra.at[dz], za_r.at[dz])
        mixed = (
            zra[0].astype(F32) + zra[1].astype(F32) + zra[2].astype(F32) + zra[3].astype(F32)
        )
        hid[...] = (entered + scale * mixed).astype(BF16)
        hidden = hid[...].astype(F32)
        first = lax.broadcasted_iota(jnp.int32, (8, tok), 0) == 0
        copies = stat_send(1, jnp.where(first, row_sums(hidden * hidden), row_sums(back[...] * hidden)))
        copies += scatter_first(hid)
        copies.append(send(hid.at[low], ad, ex_s.at[0], ex_r.at[0], 0, dp))
        au[...] = hid[high]
        totals = stat_total(1)
        scale = scale_of(totals)
        dot = totals[:, 1:2] * scale
        set_normed(hid[...], scale)
        own[...] = (
            cot[...].astype(F32) + scale * (back[...] - nrm[...].astype(F32) * dot / width)
        ).astype(BF16)
        copies += gather_own(own, 0, True)
        copies += scatter_second()
        gd[...] = own[low]
        copies += scatter_third(zrb, zb_r, False)
        writes = []
        for dz in range(4):
            for ry in range(2):
                for rx in range(2):
                    writes.append(weight_step(dz, ry, rx))
        mixed = tz[0].astype(F32)
        for dz in (1, 2, 3):
            arrived(zrb.at[dz], zb_r.at[dz])
            mixed = mixed + zrb[dz].astype(F32)
        tz[0] = (hid[...].astype(F32) + scale * mixed).astype(BF16)
        copies.append(send(tz.at[0, high], au, ex_s.at[1], ex_r.at[2], 0, dp))
        ad[...] = tz[0, low]
        arrived(gu, ex_r.at[1])
        for copy in writes:
            copy.wait()
        for copy in copies:
            copy.wait_send()


def direct_body(entering, cotangent, weights):
    streams, micro, tok_mb, cols = entering.shape
    tok = streams * micro * tok_mb
    half = tok // 2
    width = weights.shape[2]
    rows = entering.reshape(tok, cols)
    slopes = cotangent.reshape(tok, cols)
    vm = pl.BlockSpec(memory_space=pltpu.VMEM)
    hbm = pl.BlockSpec(memory_space=pl.ANY)
    half_out = jax.ShapeDtypeStruct((half, cols), BF16)
    dma = pltpu.SemaphoreType.DMA
    ad, au, gd, gu, wg = pl.pallas_call(
        window_kernel,
        out_shape=(half_out,) * 4 + (jax.ShapeDtypeStruct((cols, width), F32),),
        in_specs=[vm, vm, hbm],
        out_specs=(vm,) * 4 + (hbm,),
        scratch_shapes=[
            pltpu.VMEM((cols, width), BF16),
            pltpu.VMEM((4, 2, 2, tok, cols), BF16),
            pltpu.VMEM((4, 2, 2, tok, cols), BF16),
            pltpu.VMEM((4, 2, half, cols), BF16),
            pltpu.VMEM((4, 2, half, cols), BF16),
            pltpu.VMEM((4, half, cols), BF16),
            pltpu.VMEM((4, half, cols), BF16),
            pltpu.VMEM((4, half, cols), BF16),
            pltpu.VMEM((4, half, cols), BF16),
            pltpu.VMEM((4, tok, cols), BF16),
            pltpu.VMEM((4, tok, cols), BF16),
            pltpu.VMEM((4, tok, cols), BF16),
            pltpu.VMEM((3, 16, 8, tok), F32),
            pltpu.VMEM((tok, cols), F32),
            pltpu.VMEM((tok, cols), BF16),
            pltpu.VMEM((tok, cols), BF16),
            pltpu.VMEM((cols, tok), BF16),
            pltpu.VMEM((tok, cols), BF16),
            pltpu.VMEM((16, cols, cols), F32),
            dma, dma((16,)), dma((3, 16)), dma((3, 16)),
            dma((4, 4)), dma((4, 5)), dma((6,)),
            dma((4, 4)), dma((4, 4)), dma((4,)), dma((4,)), dma((4,)),
            dma((2,)), dma((3,)),
        ],
        compiler_params=pltpu.CompilerParams(
            collective_id=0, has_side_effects=True, vmem_limit_bytes=48 * 1024 * 1024
        ),
        cost_estimate=pl.CostEstimate(
            flops=6 * tok * cols * width, bytes_accessed=6 * cols * width, transcendentals=2 * tok
        ),
    )(rows, slopes, weights)
    shape = (1, micro, tok_mb, cols)
    return (ad.reshape(shape), au.reshape(shape), gd.reshape(shape), gu.reshape(shape), wg[None])


def solution(mesh):
    placed = (P(None, None, None, "dp"), P(None, None, None, "dp"), P("section", "dp", None))
    exact = dict(mesh.shape) == {"section": 2, "dp": 16}
    return jax.shard_map(
        direct_body if exact else body,
        mesh=mesh,
        in_specs=placed,
        out_specs=(
            P("section", None, None, "dp"),
            P("section", None, None, "dp"),
            P("section", None, None, "dp"),
            P("section", None, None, "dp"),
            P("section", "dp", None),
        ),
        check_vma=False,
    )
```

```python
import jax
import jax.numpy as jnp
from jax import lax
from jax.experimental import pallas as pl
from jax.experimental.pallas import tpu as pltpu
from jax.sharding import PartitionSpec as P

NORM_EPS = 1e-05


def for_sending(value):

    def short(part):
        return part.astype(jnp.bfloat16) if part.dtype == jnp.float32 else part

    return jax.tree.map(short, value)


def from_behind(value, axis, steps):
    count = lax.axis_size(axis)
    first, last = (max(0, -steps), min(count, count - steps))
    return lax.ppermute(value, axis, [(source, source + steps) for source in range(first, last)])


def swapped_2(block, axis, apart):
    count = lax.axis_size(axis)
    route = []
    for low in range(count):
        high = low | 1 << apart
        if high != low and high < count:
            route += [(low, high), (high, low)]
    return lax.ppermute(block, axis, route)


def pass_along(payload, ahead):
    if ahead:
        return jax.tree.map(
            lambda part, own: part.astype(own.dtype),
            from_behind(for_sending(payload), "section", 1),
            payload,
        )
    return jax.tree.map(
        lambda part, own: part.astype(own.dtype),
        from_behind(for_sending(payload), "section", -1),
        payload,
    )


def send_pair(down_part, up_part, down_ahead):
    return jnp.stack([pass_along(down_part, down_ahead), pass_along(up_part, not down_ahead)])


def section_bits():
    return lax.axis_size("section").bit_length() - 1


def mirror_weights(payload):
    for bit_idx in range(section_bits()):
        payload = swapped_2(payload, "section", bit_idx)
    return payload


def mirror_grads(payload):
    for bit_idx in range(section_bits()):
        payload = swapped_2(payload.astype(jnp.bfloat16), "section", bit_idx).astype(payload.dtype)
    return payload


def row_totals(first_part, second_part):
    return lax.psum((first_part, second_part), "dp")


def place_slot(store, stream, slot_idx, payload, is_live):
    previous = lax.dynamic_index_in_dim(store[stream], slot_idx, 0, keepdims=False)
    kept = jnp.where(is_live, payload.astype(store.dtype), previous)
    zero_idx = jnp.zeros((), jnp.int32)
    starts = (jnp.int32(stream), slot_idx) + (zero_idx,) * (store.ndim - 2)
    return lax.dynamic_update_slice(store, kept[None, None], starts)


def forward_cols(full_rows, input_cols, weight_cols):
    values = full_rows.astype(jnp.float32)
    row_scale = lax.rsqrt(jnp.mean(values * values, axis=1, keepdims=True) + NORM_EPS)
    normed = (values * row_scale).astype(jnp.bfloat16)
    mixed_cols = jnp.dot(normed, weight_cols, preferred_element_type=jnp.float32)
    output_cols = (input_cols.astype(jnp.float32) + mixed_cols).astype(jnp.bfloat16)
    return (output_cols, normed, mixed_cols, row_scale[:, 0])


def body(entering, cotangent, weights):
    section_count = lax.axis_size("section")
    last_section = section_count - 1
    section_idx = lax.axis_index("section")
    group_count = lax.axis_size("dp")
    local_cols = weights.shape[1]
    model_width = weights.shape[2]
    col_start = lax.axis_index("dp") * local_cols
    micro_count = entering.shape[1]
    tok_rows = entering.shape[2]
    tick_count = micro_count + section_count - 1
    own_rows = weights[0]
    held_rows = jnp.stack([own_rows, mirror_weights(own_rows)])
    up_delay = last_section - section_idx
    held_count = held_rows.shape[0]
    split_rows = held_rows.reshape(held_count, local_cols, group_count, local_cols)
    swapped = lax.all_to_all(split_rows, "dp", split_axis=2, concat_axis=1, tiled=True)
    held_cols = swapped.reshape(held_count, model_width, local_cols)
    held_last = held_count - 1
    fwd_delays = (section_idx, up_delay)
    back_delays = (last_section - section_idx, last_section - up_delay)

    def slot_of(tick_idx, delay_now):
        micro_idx = tick_idx - delay_now
        slot_idx = jnp.clip(micro_idx, 0, micro_count - 1)
        is_live = (micro_idx >= 0) & (micro_idx < micro_count)
        return (slot_idx, is_live)

    def forward_tick(tick_idx, state_now):
        inbox, normed_store, mixed_store, scale_store, act_store = state_now
        inputs_now = []
        slots_now = []
        for stream in range(2):
            slot_idx, is_live = slot_of(tick_idx, fwd_delays[stream])
            fresh = lax.dynamic_index_in_dim(entering[stream], slot_idx, 0, keepdims=False)
            inputs_now.append(jnp.where(fwd_delays[stream] == 0, fresh, inbox[stream]))
            slots_now.append((slot_idx, is_live))
        full_down, full_up = (
            lax.all_gather(for_sending(inputs_now[0]), "dp", axis=1, tiled=True),
            lax.all_gather(for_sending(inputs_now[1]), "dp", axis=1, tiled=True),
        )
        outputs_now = []
        for stream, full_rows in enumerate((full_down, full_up)):
            output_cols, normed, mixed_cols, row_scale = forward_cols(
                full_rows, inputs_now[stream], held_cols[stream * held_last]
            )
            slot_idx, is_live = slots_now[stream]
            normed_store = place_slot(normed_store, stream, slot_idx, normed, is_live)
            mixed_store = place_slot(mixed_store, stream, slot_idx, mixed_cols, is_live)
            scale_store = place_slot(scale_store, stream, slot_idx, row_scale, is_live)
            act_store = place_slot(act_store, stream, slot_idx, output_cols, is_live)
            outputs_now.append(output_cols)
        inbox = send_pair(outputs_now[0], outputs_now[1], True)
        return (inbox, normed_store, mixed_store, scale_store, act_store)

    start_fwd = (
        jnp.zeros((2, tok_rows, local_cols), jnp.bfloat16),
        jnp.zeros((2, micro_count, tok_rows, model_width), jnp.bfloat16),
        jnp.zeros((2, micro_count, tok_rows, local_cols), jnp.float32),
        jnp.zeros((2, micro_count, tok_rows), jnp.float32),
        jnp.zeros((2, micro_count, tok_rows, local_cols), jnp.bfloat16),
    )
    ended_fwd = lax.fori_loop(0, tick_count, forward_tick, start_fwd)
    normed_store, mixed_store, scale_store, act_store = (
        ended_fwd[1],
        ended_fwd[2],
        ended_fwd[3],
        ended_fwd[4],
    )

    def backward_tick(tick_idx, state_now):
        inbox, grad_store, weight_acc = state_now
        slopes_now = []
        picks = []
        for stream in range(2):
            slot_idx, is_live = slot_of(tick_idx, back_delays[stream])
            fresh = lax.dynamic_index_in_dim(cotangent[stream], slot_idx, 0, keepdims=False)
            slopes_now.append(jnp.where(back_delays[stream] == 0, fresh, inbox[stream]))
            normed = lax.dynamic_index_in_dim(normed_store[stream], slot_idx, 0, keepdims=False)
            mixed_cols = lax.dynamic_index_in_dim(mixed_store[stream], slot_idx, 0, keepdims=False)
            row_scale = lax.dynamic_index_in_dim(scale_store[stream], slot_idx, 0, keepdims=False)
            picks.append((slot_idx, is_live, normed, mixed_cols, row_scale))
        slope_down, slope_up = (
            lax.all_gather(for_sending(slopes_now[0]), "dp", axis=1, tiled=True),
            lax.all_gather(for_sending(slopes_now[1]), "dp", axis=1, tiled=True),
        )
        slope_fulls = (slope_down, slope_up)
        back_sums = []
        normed_locals = []
        for stream in range(2):
            back_sums.append(
                lax.dot_general(
                    slope_fulls[stream],
                    held_rows[stream * held_last],
                    (((1,), (1,)), ((), ())),
                    preferred_element_type=jnp.float32,
                )
            )
            normed_locals.append(
                lax.dynamic_slice_in_dim(picks[stream][2], col_start, local_cols, 1)
            )
        row_sums = row_totals(
            jnp.sum(back_sums[0] * normed_locals[0].astype(jnp.float32), axis=1),
            jnp.sum(back_sums[1] * normed_locals[1].astype(jnp.float32), axis=1),
        )
        grads_now = []
        for stream in range(2):
            slot_idx, is_live, normed, mixed_cols, row_scale = picks[stream]
            row_dot = row_sums[stream][:, None]
            normed_part = normed_locals[stream].astype(jnp.float32)
            grad_cols = (
                slopes_now[stream].astype(jnp.float32)
                + row_scale[:, None] * (back_sums[stream] - normed_part * row_dot / model_width)
            ).astype(jnp.bfloat16)
            weight_step = lax.dot_general(
                normed_locals[stream],
                slope_fulls[stream],
                (((0,), (0,)), ((), ())),
                preferred_element_type=jnp.float32,
            )
            weight_acc = weight_acc.at[stream].add(weight_step * is_live.astype(jnp.float32))
            grad_store = place_slot(grad_store, stream, slot_idx, grad_cols, is_live)
            grads_now.append(grad_cols)
        inbox = send_pair(grads_now[0], grads_now[1], False)
        return (inbox, grad_store, weight_acc)

    start_back = (
        jnp.zeros((2, tok_rows, local_cols), jnp.bfloat16),
        jnp.zeros((2, micro_count, tok_rows, local_cols), jnp.bfloat16),
        jnp.zeros((2, local_cols, model_width), jnp.float32),
    )
    ended_back = lax.fori_loop(0, tick_count, backward_tick, start_back)
    grad_store, weight_acc = (ended_back[1], ended_back[2])
    total_grad = weight_acc[0] + mirror_grads(weight_acc[1])
    acts_up = act_store[1]
    grads_up = grad_store[1]
    return (
        act_store[0][None],
        acts_up[None],
        grad_store[0][None],
        grads_up[None],
        total_grad[None],
    )


MESH = pl.DeviceIdType.MESH
F32 = jnp.float32
BF16 = jnp.bfloat16
Z_ORDER = (1, 3, 2, 0)


def row_sums(values):
    ones = jnp.ones((8, values.shape[1]), F32)
    return lax.dot_general(
        ones,
        values,
        (((1,), (1,)), ((), ())),
        precision=lax.Precision.HIGHEST,
        preferred_element_type=F32,
    )


def window_kernel(
    h0_hbm, cot_hbm, w_hbm, ad, au, gd, gu, nrm_t, gf_hbm,
    h0, cot, w, gf, part, a1, b1, a2, b2, sa, sb, tz, zra, zrb, stats, back, hid, nrm, own,
    in_sem, keep_sem, st_s, st_r, ag_s, ag_r, own_s, rs_s, rs_r, z_s, za_r, zb_r, ex_s, ex_r,
):
    tok, cols = h0.shape
    half = tok // 2
    low, high = pl.ds(0, half), pl.ds(half, half)
    width = cols * 16
    sec = lax.axis_index("section")
    dp = lax.axis_index("dp")
    z, y, x = dp // 4, (dp // 2) % 2, dp % 2
    px, py = dp + 1 - 2 * x, dp + 2 - 4 * y

    def zp(dz):
        return ((z + dz) % 4) * 4 + y * 2 + x

    def block_cols(dz, ry, rx):
        yy = 1 - y if ry else y
        xx = 1 - x if rx else x
        return pl.ds(pl.multiple_of((((z + dz) % 4) * 4 + yy * 2 + xx) * cols, cols), cols)

    def send(src, dst, s_sem, r_sem, section, chip):
        copy = pltpu.make_async_remote_copy(
            src_ref=src, dst_ref=dst, send_sem=s_sem, recv_sem=r_sem,
            device_id=(section, chip), device_id_type=MESH,
        )
        copy.start()
        return copy

    def arrived(dst, r_sem):
        pltpu.make_async_remote_copy(
            src_ref=dst, dst_ref=dst, send_sem=r_sem, recv_sem=r_sem,
            device_id=(sec, dp), device_id_type=MESH,
        ).wait_recv()

    load_h = pltpu.make_async_copy(h0_hbm, h0, in_sem.at[0])
    load_h.start()
    load_c = pltpu.make_async_copy(cot_hbm, cot, in_sem.at[1])
    load_c.start()
    load_w = pltpu.make_async_copy(w_hbm.at[0], w, in_sem.at[2])
    load_w.start()

    barrier = pltpu.get_barrier_semaphore()
    for step in range(1, 16):
        pl.semaphore_signal(barrier, inc=1, device_id=(sec, (dp + step) % 16), device_id_type=MESH)
    for chip in (dp, px, py, zp(1), zp(2), zp(3)):
        pl.semaphore_signal(barrier, inc=1, device_id=(1 - sec, chip), device_id_type=MESH)
    pl.semaphore_wait(barrier, 21)

    def stat_send(k, value):
        stats[k, dp] = value[0:2]
        copies = []
        for step in range(1, 16):
            copies.append(send(
                stats.at[k, dp], stats.at[k, dp], st_s.at[k, step], st_r.at[k, step],
                sec, (dp + step) % 16,
            ))
        return copies

    def stat_total(k):
        for step in range(1, 16):
            arrived(stats.at[k, (dp + 16 - step) % 16], st_r.at[k, step])
        total = jnp.sum(stats[k], axis=0)
        return jnp.transpose(jnp.concatenate([total] * 4, axis=0))

    def gather_own(src, section, include_self):
        copies = []
        for dz in (1, 2, 3):
            copies.append(send(src, gf.at[4 - dz, 0, 0], own_s.at[dz], ag_r.at[4 - dz, 0], section, zp(dz)))
        copies.append(send(src, gf.at[0, 0, 1], own_s.at[4], ag_r.at[0, 1], section, px))
        copies.append(send(src, gf.at[0, 1, 0], own_s.at[5], ag_r.at[0, 2], section, py))
        if include_self:
            copies.append(send(src, gf.at[0, 0, 0], own_s.at[0], ag_r.at[0, 0], section, dp))
        return copies

    def gather_rest(use, own_arrives):
        copies = []
        for dz in (1, 3, 2):
            arrived(gf.at[dz, 0, 0], ag_r.at[dz, 0])
            copies.append(send(gf.at[dz, 0, 0], gf.at[dz, 0, 1], ag_s.at[dz, 0], ag_r.at[dz, 1], sec, px))
            copies.append(send(gf.at[dz, 0, 0], gf.at[dz, 1, 0], ag_s.at[dz, 1], ag_r.at[dz, 2], sec, py))
            if dz == 1:
                if own_arrives:
                    arrived(gf.at[0, 0, 0], ag_r.at[0, 0])
                use(0, 0, 0)
            use(dz, 0, 0)
        for dz in (0, 1, 3, 2):
            arrived(gf.at[dz, 0, 1], ag_r.at[dz, 1])
            copies.append(send(
                gf.at[dz, 0, 1, low], gf.at[dz, 1, 1, low], ag_s.at[dz, 2], ag_r.at[dz, 3], sec, py))
            arrived(gf.at[dz, 1, 0], ag_r.at[dz, 2])
            copies.append(send(
                gf.at[dz, 1, 0, high], gf.at[dz, 1, 1, high], ag_s.at[dz, 3], ag_r.at[dz, 4], sec, px))
            use(dz, 0, 1)
            use(dz, 1, 0)
        for dz in (0, 1, 3, 2):
            arrived(gf.at[dz, 1, 1, low], ag_r.at[dz, 3])
            arrived(gf.at[dz, 1, 1, high], ag_r.at[dz, 4])
            use(dz, 1, 1)
        return copies

    def scatter_first(rows, order):
        copies = []
        for dz in order:
            for ry, rx in ((0, 1), (1, 1), (1, 0), (0, 0)):
                part[dz, ry, rx] = jnp.dot(
                    rows[...], w[:, block_cols(dz, ry, rx)], preferred_element_type=F32
                ).astype(BF16)
                if (ry, rx) == (1, 1):
                    copies.append(send(
                        part.at[dz, pl.ds(0, 2), 1, low], a1.at[dz], rs_s.at[dz, 0], rs_r.at[dz, 0], sec, px))
                if (ry, rx) == (1, 0):
                    copies.append(send(
                        part.at[dz, 1, pl.ds(0, 2), high], b1.at[dz], rs_s.at[dz, 1], rs_r.at[dz, 1], sec, py))
        return copies

    def scatter_second():
        copies = []
        for dz in Z_ORDER:
            arrived(a1.at[dz], rs_r.at[dz, 0])
            sa[dz] = (part[dz, 1, 0, low].astype(F32) + a1[dz, 1].astype(F32)).astype(BF16)
            copies.append(send(sa.at[dz], a2.at[dz], rs_s.at[dz, 2], rs_r.at[dz, 2], sec, py))
            arrived(b1.at[dz], rs_r.at[dz, 1])
            sb[dz] = (part[dz, 0, 1, high].astype(F32) + b1[dz, 1].astype(F32)).astype(BF16)
            copies.append(send(sb.at[dz], b2.at[dz], rs_s.at[dz, 3], rs_r.at[dz, 3], sec, px))
        return copies

    def scatter_third(landing, r_sems, self_too):
        copies = []
        for dz in Z_ORDER:
            arrived(a2.at[dz], rs_r.at[dz, 2])
            tz[dz, low] = (
                part[dz, 0, 0, low].astype(F32) + a1[dz, 0].astype(F32) + a2[dz].astype(F32)
            ).astype(BF16)
            arrived(b2.at[dz], rs_r.at[dz, 3])
            tz[dz, high] = (
                part[dz, 0, 0, high].astype(F32) + b1[dz, 0].astype(F32) + b2[dz].astype(F32)
            ).astype(BF16)
            if dz:
                copies.append(send(tz.at[dz], landing.at[4 - dz], z_s.at[dz], r_sems.at[4 - dz], 1, zp(dz)))
            elif self_too:
                copies.append(send(tz.at[0], landing.at[0], z_s.at[0], r_sems.at[0], 1, dp))
        return copies

    def back_step(dz, ry, rx):
        return lax.dot_general(
            gf[dz, ry, rx], w[:, block_cols(dz, ry, rx)], (((1,), (1,)), ((), ())),
            preferred_element_type=F32,
        )

    def keep(dz, ry, rx):
        copy = pltpu.make_async_copy(
            gf.at[dz, ry, rx], gf_hbm.at[dz, ry, rx], keep_sem.at[dz * 4 + ry * 2 + rx])
        copy.start()
        return copy

    def scale_of(totals):
        return lax.rsqrt(totals[:, 0:1] / width + NORM_EPS)

    def set_normed(values, scale):
        normed = values.astype(F32) * scale
        nrm[...] = normed.astype(BF16)
        nrm_t[...] = jnp.transpose(normed).astype(BF16)

    @pl.when(sec == 0)
    def _():
        load_h.wait()
        entered = h0[...].astype(F32)
        copies = stat_send(0, row_sums(entered * entered))
        load_w.wait()
        copies += scatter_first(h0, Z_ORDER)
        load_c.wait()
        copies += scatter_second()
        copies += scatter_third(zra, za_r, True)
        scale = scale_of(stat_total(0))
        set_normed(h0[...], scale)
        back[...] = jnp.zeros_like(back)
        writes = []

        def use(dz, ry, rx):
            back[...] += back_step(dz, ry, rx)
            writes.append(keep(dz, ry, rx))

        copies += gather_rest(use, True)
        normed = nrm[...].astype(F32)
        copies += stat_send(2, row_sums(back[...] * normed))
        gu[...] = gf[0, 0, 0, high]
        arrived(ad, ex_r.at[0])
        dot = stat_total(2)[:, 0:1]
        own[...] = (
            gf[0, 0, 0].astype(F32) + scale * (back[...] - normed * dot / width)
        ).astype(BF16)
        copies.append(send(own.at[high], gu, ex_s.at[0], ex_r.at[1], 1, dp))
        gd[...] = own[low]
        arrived(au, ex_r.at[2])
        for copy in writes:
            copy.wait()
        for copy in copies:
            copy.wait_send()

    @pl.when(sec == 1)
    def _():
        load_c.wait()
        copies = gather_own(cot, 1, False)
        gf[0, 0, 0] = cot[...]
        load_h.wait()
        entered = h0[...].astype(F32)
        copies += stat_send(0, row_sums(entered * entered))
        back[...] = jnp.zeros_like(back)
        load_w.wait()

        writes = []

        def use(dz, ry, rx):
            back[...] += back_step(dz, ry, rx)
            writes.append(keep(dz, ry, rx))

        copies += gather_rest(use, False)
        for copy in copies:
            copy.wait_send()
        scale = scale_of(stat_total(0))
        for dz in (0, 1, 3, 2):
            arrived(zra.at[dz], za_r.at[dz])
        mixed = (
            zra[0].astype(F32) + zra[1].astype(F32) + zra[2].astype(F32) + zra[3].astype(F32)
        )
        hid[...] = (entered + scale * mixed).astype(BF16)
        hidden = hid[...].astype(F32)
        first = lax.broadcasted_iota(jnp.int32, (8, tok), 0) == 0
        copies = stat_send(1, jnp.where(first, row_sums(hidden * hidden), row_sums(back[...] * hidden)))
        copies += scatter_first(hid, Z_ORDER[:2])
        copies.append(send(hid.at[low], ad, ex_s.at[0], ex_r.at[0], 0, dp))
        au[...] = hid[high]
        totals = stat_total(1)
        scale = scale_of(totals)
        dot = totals[:, 1:2] * scale
        set_normed(hid[...], scale)
        own[...] = (
            cot[...].astype(F32) + scale * (back[...] - nrm[...].astype(F32) * dot / width)
        ).astype(BF16)
        copies += gather_own(own, 0, True)
        copies += scatter_first(hid, Z_ORDER[2:])
        copies += scatter_second()
        gd[...] = own[low]
        copies += scatter_third(zrb, zb_r, False)
        mixed = tz[0].astype(F32)
        for dz in (1, 2, 3):
            arrived(zrb.at[dz], zb_r.at[dz])
            mixed = mixed + zrb[dz].astype(F32)
        tz[0] = (hid[...].astype(F32) + scale * mixed).astype(BF16)
        copies.append(send(tz.at[0, high], au, ex_s.at[1], ex_r.at[2], 0, dp))
        ad[...] = tz[0, low]
        arrived(gu, ex_r.at[1])
        for copy in writes:
            copy.wait()
        for copy in copies:
            copy.wait_send()


def finish_kernel(nrm_t, gf_hbm, *refs):
    kept, outs, (wg_hbm, gf, wg, in_sem, wg_sem, out_sem) = refs[:4], refs[4:8], refs[8:]
    cols = nrm_t.shape[0]
    dp = lax.axis_index("dp")
    z, y, x = dp // 4, (dp // 2) % 2, dp % 2
    loads, copies = [], []
    for k in range(16):
        spot = (k // 4, (k // 2) % 2, k % 2)
        loads.append(pltpu.make_async_copy(gf_hbm.at[spot], gf.at[k], in_sem.at[k]))
        loads[k].start()
    for k in range(4):
        copies.append(pltpu.make_async_copy(kept[k], outs[k], out_sem.at[k]))
        copies[k].start()
    for k in range(16):
        loads[k].wait()
        yy = 1 - y if (k // 2) % 2 else y
        xx = 1 - x if k % 2 else x
        block = ((z + k // 4) % 4) * 4 + yy * 2 + xx
        wg[k] = jnp.dot(nrm_t[...], gf[k], preferred_element_type=F32)
        spot = pl.ds(pl.multiple_of(block * cols, cols), cols)
        copy = pltpu.make_async_copy(wg.at[k], wg_hbm.at[:, spot], wg_sem.at[k])
        copy.start()
        copies.append(copy)
    for copy in copies:
        copy.wait()


def direct_body(entering, cotangent, weights):
    streams, micro, tok_mb, cols = entering.shape
    tok = streams * micro * tok_mb
    half = tok // 2
    width = weights.shape[2]
    rows = entering.reshape(tok, cols)
    slopes = cotangent.reshape(tok, cols)
    vm = pl.BlockSpec(memory_space=pltpu.VMEM)
    hbm = pl.BlockSpec(memory_space=pl.ANY)
    half_out = jax.ShapeDtypeStruct((half, cols), BF16)
    dma = pltpu.SemaphoreType.DMA
    *kept, nrm_t, gathered = pl.pallas_call(
        window_kernel,
        out_shape=(half_out,) * 4 + (
            jax.ShapeDtypeStruct((cols, tok), BF16),
            jax.ShapeDtypeStruct((4, 2, 2, tok, cols), BF16),
        ),
        in_specs=[hbm, hbm, hbm],
        out_specs=(vm,) * 5 + (hbm,),
        scratch_shapes=[
            pltpu.VMEM((tok, cols), BF16),
            pltpu.VMEM((tok, cols), BF16),
            pltpu.VMEM((cols, width), BF16),
            pltpu.VMEM((4, 2, 2, tok, cols), BF16),
            pltpu.VMEM((4, 2, 2, tok, cols), BF16),
            pltpu.VMEM((4, 2, half, cols), BF16),
            pltpu.VMEM((4, 2, half, cols), BF16),
            pltpu.VMEM((4, half, cols), BF16),
            pltpu.VMEM((4, half, cols), BF16),
            pltpu.VMEM((4, half, cols), BF16),
            pltpu.VMEM((4, half, cols), BF16),
            pltpu.VMEM((4, tok, cols), BF16),
            pltpu.VMEM((4, tok, cols), BF16),
            pltpu.VMEM((4, tok, cols), BF16),
            pltpu.VMEM((3, 16, 2, tok), F32),
            pltpu.VMEM((tok, cols), F32),
            pltpu.VMEM((tok, cols), BF16),
            pltpu.VMEM((tok, cols), BF16),
            pltpu.VMEM((tok, cols), BF16),
            dma((3,)), dma((16,)), dma((3, 16)), dma((3, 16)),
            dma((4, 4)), dma((4, 5)), dma((6,)),
            dma((4, 4)), dma((4, 4)), dma((4,)), dma((4,)), dma((4,)),
            dma((2,)), dma((3,)),
        ],
        compiler_params=pltpu.CompilerParams(
            collective_id=0, has_side_effects=True, vmem_limit_bytes=63 * 1024 * 1024
        ),
        cost_estimate=pl.CostEstimate(
            flops=4 * tok * cols * width, bytes_accessed=4 * cols * width, transcendentals=2 * tok
        ),
    )(rows, slopes, weights)
    *outs, weight_grad = pl.pallas_call(
        finish_kernel,
        out_shape=(half_out,) * 4 + (jax.ShapeDtypeStruct((cols, width), F32),),
        in_specs=[vm, hbm] + [vm] * 4,
        out_specs=(hbm,) * 5,
        scratch_shapes=[
            pltpu.VMEM((16, tok, cols), BF16),
            pltpu.VMEM((16, cols, cols), F32),
            dma((16,)), dma((16,)), dma((4,)),
        ],
        compiler_params=pltpu.CompilerParams(vmem_limit_bytes=63 * 1024 * 1024),
        cost_estimate=pl.CostEstimate(
            flops=2 * tok * cols * width, bytes_accessed=6 * cols * width, transcendentals=0
        ),
    )(nrm_t, gathered, *kept)
    shape = (1, micro, tok_mb, cols)
    return (*(out.reshape(shape) for out in outs), weight_grad[None])


def solution(mesh):
    placed = (P(None, None, None, "dp"), P(None, None, None, "dp"), P("section", "dp", None))
    exact = dict(mesh.shape) == {"section": 2, "dp": 16}
    return jax.shard_map(
        direct_body if exact else body,
        mesh=mesh,
        in_specs=placed,
        out_specs=(
            P("section", None, None, "dp"),
            P("section", None, None, "dp"),
            P("section", None, None, "dp"),
            P("section", None, None, "dp"),
            P("section", "dp", None),
        ),
        check_vma=False,
    )
```

```python
import jax
import jax.numpy as jnp
from jax import lax
from jax.experimental import pallas as pl
from jax.experimental.pallas import tpu as pltpu
from jax.sharding import PartitionSpec as P

NORM_EPS = 1e-05


def for_sending(value):

    def short(part):
        return part.astype(jnp.bfloat16) if part.dtype == jnp.float32 else part

    return jax.tree.map(short, value)


def from_behind(value, axis, steps):
    count = lax.axis_size(axis)
    first, last = (max(0, -steps), min(count, count - steps))
    return lax.ppermute(value, axis, [(source, source + steps) for source in range(first, last)])


def swapped_2(block, axis, apart):
    count = lax.axis_size(axis)
    route = []
    for low in range(count):
        high = low | 1 << apart
        if high != low and high < count:
            route += [(low, high), (high, low)]
    return lax.ppermute(block, axis, route)


def pass_along(payload, ahead):
    if ahead:
        return jax.tree.map(
            lambda part, own: part.astype(own.dtype),
            from_behind(for_sending(payload), "section", 1),
            payload,
        )
    return jax.tree.map(
        lambda part, own: part.astype(own.dtype),
        from_behind(for_sending(payload), "section", -1),
        payload,
    )


def send_pair(down_part, up_part, down_ahead):
    return jnp.stack([pass_along(down_part, down_ahead), pass_along(up_part, not down_ahead)])


def section_bits():
    return lax.axis_size("section").bit_length() - 1


def mirror_weights(payload):
    for bit_idx in range(section_bits()):
        payload = swapped_2(payload, "section", bit_idx)
    return payload


def mirror_grads(payload):
    for bit_idx in range(section_bits()):
        payload = swapped_2(payload.astype(jnp.bfloat16), "section", bit_idx).astype(payload.dtype)
    return payload


def row_totals(first_part, second_part):
    return lax.psum((first_part, second_part), "dp")


def place_slot(store, stream, slot_idx, payload, is_live):
    previous = lax.dynamic_index_in_dim(store[stream], slot_idx, 0, keepdims=False)
    kept = jnp.where(is_live, payload.astype(store.dtype), previous)
    zero_idx = jnp.zeros((), jnp.int32)
    starts = (jnp.int32(stream), slot_idx) + (zero_idx,) * (store.ndim - 2)
    return lax.dynamic_update_slice(store, kept[None, None], starts)


def forward_cols(full_rows, input_cols, weight_cols):
    values = full_rows.astype(jnp.float32)
    row_scale = lax.rsqrt(jnp.mean(values * values, axis=1, keepdims=True) + NORM_EPS)
    normed = (values * row_scale).astype(jnp.bfloat16)
    mixed_cols = jnp.dot(normed, weight_cols, preferred_element_type=jnp.float32)
    output_cols = (input_cols.astype(jnp.float32) + mixed_cols).astype(jnp.bfloat16)
    return (output_cols, normed, mixed_cols, row_scale[:, 0])


def body(entering, cotangent, weights):
    section_count = lax.axis_size("section")
    last_section = section_count - 1
    section_idx = lax.axis_index("section")
    group_count = lax.axis_size("dp")
    local_cols = weights.shape[1]
    model_width = weights.shape[2]
    col_start = lax.axis_index("dp") * local_cols
    micro_count = entering.shape[1]
    tok_rows = entering.shape[2]
    tick_count = micro_count + section_count - 1
    own_rows = weights[0]
    held_rows = jnp.stack([own_rows, mirror_weights(own_rows)])
    up_delay = last_section - section_idx
    held_count = held_rows.shape[0]
    split_rows = held_rows.reshape(held_count, local_cols, group_count, local_cols)
    swapped = lax.all_to_all(split_rows, "dp", split_axis=2, concat_axis=1, tiled=True)
    held_cols = swapped.reshape(held_count, model_width, local_cols)
    held_last = held_count - 1
    fwd_delays = (section_idx, up_delay)
    back_delays = (last_section - section_idx, last_section - up_delay)

    def slot_of(tick_idx, delay_now):
        micro_idx = tick_idx - delay_now
        slot_idx = jnp.clip(micro_idx, 0, micro_count - 1)
        is_live = (micro_idx >= 0) & (micro_idx < micro_count)
        return (slot_idx, is_live)

    def forward_tick(tick_idx, state_now):
        inbox, normed_store, mixed_store, scale_store, act_store = state_now
        inputs_now = []
        slots_now = []
        for stream in range(2):
            slot_idx, is_live = slot_of(tick_idx, fwd_delays[stream])
            fresh = lax.dynamic_index_in_dim(entering[stream], slot_idx, 0, keepdims=False)
            inputs_now.append(jnp.where(fwd_delays[stream] == 0, fresh, inbox[stream]))
            slots_now.append((slot_idx, is_live))
        full_down, full_up = (
            lax.all_gather(for_sending(inputs_now[0]), "dp", axis=1, tiled=True),
            lax.all_gather(for_sending(inputs_now[1]), "dp", axis=1, tiled=True),
        )
        outputs_now = []
        for stream, full_rows in enumerate((full_down, full_up)):
            output_cols, normed, mixed_cols, row_scale = forward_cols(
                full_rows, inputs_now[stream], held_cols[stream * held_last]
            )
            slot_idx, is_live = slots_now[stream]
            normed_store = place_slot(normed_store, stream, slot_idx, normed, is_live)
            mixed_store = place_slot(mixed_store, stream, slot_idx, mixed_cols, is_live)
            scale_store = place_slot(scale_store, stream, slot_idx, row_scale, is_live)
            act_store = place_slot(act_store, stream, slot_idx, output_cols, is_live)
            outputs_now.append(output_cols)
        inbox = send_pair(outputs_now[0], outputs_now[1], True)
        return (inbox, normed_store, mixed_store, scale_store, act_store)

    start_fwd = (
        jnp.zeros((2, tok_rows, local_cols), jnp.bfloat16),
        jnp.zeros((2, micro_count, tok_rows, model_width), jnp.bfloat16),
        jnp.zeros((2, micro_count, tok_rows, local_cols), jnp.float32),
        jnp.zeros((2, micro_count, tok_rows), jnp.float32),
        jnp.zeros((2, micro_count, tok_rows, local_cols), jnp.bfloat16),
    )
    ended_fwd = lax.fori_loop(0, tick_count, forward_tick, start_fwd)
    normed_store, mixed_store, scale_store, act_store = (
        ended_fwd[1],
        ended_fwd[2],
        ended_fwd[3],
        ended_fwd[4],
    )

    def backward_tick(tick_idx, state_now):
        inbox, grad_store, weight_acc = state_now
        slopes_now = []
        picks = []
        for stream in range(2):
            slot_idx, is_live = slot_of(tick_idx, back_delays[stream])
            fresh = lax.dynamic_index_in_dim(cotangent[stream], slot_idx, 0, keepdims=False)
            slopes_now.append(jnp.where(back_delays[stream] == 0, fresh, inbox[stream]))
            normed = lax.dynamic_index_in_dim(normed_store[stream], slot_idx, 0, keepdims=False)
            mixed_cols = lax.dynamic_index_in_dim(mixed_store[stream], slot_idx, 0, keepdims=False)
            row_scale = lax.dynamic_index_in_dim(scale_store[stream], slot_idx, 0, keepdims=False)
            picks.append((slot_idx, is_live, normed, mixed_cols, row_scale))
        slope_down, slope_up = (
            lax.all_gather(for_sending(slopes_now[0]), "dp", axis=1, tiled=True),
            lax.all_gather(for_sending(slopes_now[1]), "dp", axis=1, tiled=True),
        )
        slope_fulls = (slope_down, slope_up)
        back_sums = []
        normed_locals = []
        for stream in range(2):
            back_sums.append(
                lax.dot_general(
                    slope_fulls[stream],
                    held_rows[stream * held_last],
                    (((1,), (1,)), ((), ())),
                    preferred_element_type=jnp.float32,
                )
            )
            normed_locals.append(
                lax.dynamic_slice_in_dim(picks[stream][2], col_start, local_cols, 1)
            )
        row_sums = row_totals(
            jnp.sum(back_sums[0] * normed_locals[0].astype(jnp.float32), axis=1),
            jnp.sum(back_sums[1] * normed_locals[1].astype(jnp.float32), axis=1),
        )
        grads_now = []
        for stream in range(2):
            slot_idx, is_live, normed, mixed_cols, row_scale = picks[stream]
            row_dot = row_sums[stream][:, None]
            normed_part = normed_locals[stream].astype(jnp.float32)
            grad_cols = (
                slopes_now[stream].astype(jnp.float32)
                + row_scale[:, None] * (back_sums[stream] - normed_part * row_dot / model_width)
            ).astype(jnp.bfloat16)
            weight_step = lax.dot_general(
                normed_locals[stream],
                slope_fulls[stream],
                (((0,), (0,)), ((), ())),
                preferred_element_type=jnp.float32,
            )
            weight_acc = weight_acc.at[stream].add(weight_step * is_live.astype(jnp.float32))
            grad_store = place_slot(grad_store, stream, slot_idx, grad_cols, is_live)
            grads_now.append(grad_cols)
        inbox = send_pair(grads_now[0], grads_now[1], False)
        return (inbox, grad_store, weight_acc)

    start_back = (
        jnp.zeros((2, tok_rows, local_cols), jnp.bfloat16),
        jnp.zeros((2, micro_count, tok_rows, local_cols), jnp.bfloat16),
        jnp.zeros((2, local_cols, model_width), jnp.float32),
    )
    ended_back = lax.fori_loop(0, tick_count, backward_tick, start_back)
    grad_store, weight_acc = (ended_back[1], ended_back[2])
    total_grad = weight_acc[0] + mirror_grads(weight_acc[1])
    acts_up = act_store[1]
    grads_up = grad_store[1]
    return (
        act_store[0][None],
        acts_up[None],
        grad_store[0][None],
        grads_up[None],
        total_grad[None],
    )


MESH = pl.DeviceIdType.MESH
F32 = jnp.float32
BF16 = jnp.bfloat16
EARLY = 2


def row_sums(values):
    ones = jnp.ones((8, values.shape[1]), F32)
    return lax.dot_general(
        ones,
        values,
        (((1,), (1,)), ((), ())),
        precision=lax.Precision.HIGHEST,
        preferred_element_type=F32,
    )


def peer_block(dp, dz, ry, rx):
    z, y, x = dp // 4, (dp // 2) % 2, dp % 2
    return ((z + dz) % 4) * 4 + ((y + ry) % 2) * 2 + (x + rx) % 2


def each(low, high, step):
    lax.fori_loop(low, high, lambda i, carry: (step(i), carry)[1], 0)


def window_kernel(
    h0_hbm, cot_hbm, w_hbm, ad, au, gd, gu, nrm_t, gf_hbm,
    h0, cot, w, gf, part, a1, b1, a2, b2, sa, sb, tz, zra, zrb, stats, back, hid, nrm, own,
    in_sem, keep_sem, st_s, st_r, ag_s, ag_r, own_s, rs_s, rs_r, z_s, za_r, zb_r, ex_s, ex_r,
):
    tok, cols = h0.shape
    half = tok // 2
    low, high = pl.ds(0, half), pl.ds(half, half)
    width = cols * 16
    sec = lax.axis_index("section")
    dp = lax.axis_index("dp")
    px, py = peer_block(dp, 0, 0, 1), peer_block(dp, 0, 1, 0)

    def zp(dz):
        return peer_block(dp, dz, 0, 0)

    def block_cols(dz, ry, rx):
        return pl.ds(pl.multiple_of(peer_block(dp, dz, ry, rx) * cols, cols), cols)

    def remote(src, dst, s_sem, r_sem, section, chip):
        return pltpu.make_async_remote_copy(
            src_ref=src, dst_ref=dst, send_sem=s_sem, recv_sem=r_sem,
            device_id=(section, chip), device_id_type=MESH,
        )

    def send(*args):
        remote(*args).start()

    def arrived(dst, r_sem):
        remote(dst, dst, r_sem, r_sem, sec, dp).wait_recv()

    def sent(src, s_sem):
        remote(src, src, s_sem, s_sem, sec, dp).wait_send()

    load_h = pltpu.make_async_copy(h0_hbm, h0, in_sem.at[0])
    load_h.start()
    load_c = pltpu.make_async_copy(cot_hbm, cot, in_sem.at[1])
    load_c.start()
    load_w = pltpu.make_async_copy(w_hbm.at[0], w, in_sem.at[2])
    load_w.start()

    barrier = pltpu.get_barrier_semaphore()

    def greet(section, chip):
        pl.semaphore_signal(barrier, inc=1, device_id=(section, chip), device_id_type=MESH)

    each(1, 16, lambda step: greet(sec, (dp + step) % 16))
    for chip in (dp, px, py, zp(1), zp(2), zp(3)):
        greet(1 - sec, chip)
    pl.semaphore_wait(barrier, 21)

    def stat_send(k, value):
        stats[k, dp] = value[0:2]
        each(1, 16, lambda step: send(
            stats.at[k, dp], stats.at[k, dp], st_s.at[k, step], st_r.at[k, step],
            sec, (dp + step) % 16,
        ))

    def stat_total(k):
        each(1, 16, lambda step: arrived(stats.at[k, (dp + 16 - step) % 16], st_r.at[k, step]))
        total = jnp.sum(stats[k], axis=0)
        return jnp.transpose(jnp.concatenate([total] * 4, axis=0))

    def stat_sent(k):
        each(1, 16, lambda step: sent(stats.at[k, dp], st_s.at[k, step]))

    def gather_own(src, section, include_self):
        for dz in (1, 2, 3):
            send(src, gf.at[4 - dz, 0, 0], own_s.at[dz], ag_r.at[4 - dz, 0], section, zp(dz))
        send(src, gf.at[0, 0, 1], own_s.at[4], ag_r.at[0, 1], section, px)
        send(src, gf.at[0, 1, 0], own_s.at[5], ag_r.at[0, 2], section, py)
        if include_self:
            send(src, gf.at[0, 0, 0], own_s.at[0], ag_r.at[0, 0], section, dp)

    def own_sent(src, include_self):
        each(0 if include_self else 1, 6, lambda k: sent(src, own_s.at[k]))

    def kept(dz, ry, rx):
        return pltpu.make_async_copy(
            gf.at[dz, ry, rx], gf_hbm.at[dz, ry, rx], keep_sem.at[dz * 4 + ry * 2 + rx])

    def use(dz, ry, rx):
        kept(dz, ry, rx).start()
        back[...] += lax.dot_general(
            gf[dz, ry, rx], w[:, block_cols(dz, ry, rx)], (((1,), (1,)), ((), ())),
            preferred_element_type=F32,
        )

    def gather_rest(own_arrives):
        back[...] = jnp.zeros_like(back)

        def along_z(i):
            dz = (i + 1) % 4

            @pl.when(dz != 0)
            def _():
                arrived(gf.at[dz, 0, 0], ag_r.at[dz, 0])
                send(gf.at[dz, 0, 0], gf.at[dz, 0, 1], ag_s.at[dz, 0], ag_r.at[dz, 1], sec, px)
                send(gf.at[dz, 0, 0], gf.at[dz, 1, 0], ag_s.at[dz, 1], ag_r.at[dz, 2], sec, py)

            if own_arrives:
                @pl.when(dz == 0)
                def _():
                    arrived(gf.at[0, 0, 0], ag_r.at[0, 0])

            use(dz, 0, 0)

        def across(dz):
            arrived(gf.at[dz, 0, 1], ag_r.at[dz, 1])
            send(gf.at[dz, 0, 1, low], gf.at[dz, 1, 1, low], ag_s.at[dz, 2], ag_r.at[dz, 3], sec, py)
            arrived(gf.at[dz, 1, 0], ag_r.at[dz, 2])
            send(gf.at[dz, 1, 0, high], gf.at[dz, 1, 1, high], ag_s.at[dz, 3], ag_r.at[dz, 4], sec, px)
            each(0, 2, lambda k: use(dz, k, 1 - k))

        def diagonal(dz):
            arrived(gf.at[dz, 1, 1, low], ag_r.at[dz, 3])
            arrived(gf.at[dz, 1, 1, high], ag_r.at[dz, 4])
            use(dz, 1, 1)

        each(0, 4, along_z)
        each(0, 4, across)
        each(0, 4, diagonal)

    def rest_sent():
        def forwarded(dz):
            sent(gf.at[dz, 0, 0], ag_s.at[dz, 0])
            sent(gf.at[dz, 0, 0], ag_s.at[dz, 1])

        def halves(dz):
            sent(gf.at[dz, 0, 1, low], ag_s.at[dz, 2])
            sent(gf.at[dz, 1, 0, high], ag_s.at[dz, 3])

        each(1, 4, forwarded)
        each(0, 4, halves)
        each(0, 16, lambda k: kept(k // 4, (k // 2) % 2, k % 2).wait())

    def scatter_first(rows, start, stop):
        def step(k):
            dz, j = (k // 4 + 1) % 4, k % 4
            ry, rx = 1 - j % 2, 1 - j // 2
            part[dz, ry, rx] = jnp.dot(
                rows[...], w[:, block_cols(dz, ry, rx)], preferred_element_type=F32
            ).astype(BF16)

            @pl.when(j == 1)
            def _():
                send(part.at[dz, pl.ds(0, 2), 1, low], a1.at[dz], rs_s.at[dz, 0], rs_r.at[dz, 0], sec, px)

            @pl.when(j == 2)
            def _():
                send(part.at[dz, 1, pl.ds(0, 2), high], b1.at[dz], rs_s.at[dz, 1], rs_r.at[dz, 1], sec, py)

        each(4 * start, 4 * stop, step)

    def scatter_rest(landing, r_sems, self_too):
        def second(i):
            dz = (i + 1) % 4
            arrived(a1.at[dz], rs_r.at[dz, 0])
            sa[dz] = (part[dz, 1, 0, low].astype(F32) + a1[dz, 1].astype(F32)).astype(BF16)
            send(sa.at[dz], a2.at[dz], rs_s.at[dz, 2], rs_r.at[dz, 2], sec, py)
            arrived(b1.at[dz], rs_r.at[dz, 1])
            sb[dz] = (part[dz, 0, 1, high].astype(F32) + b1[dz, 1].astype(F32)).astype(BF16)
            send(sb.at[dz], b2.at[dz], rs_s.at[dz, 3], rs_r.at[dz, 3], sec, px)

        def third(i):
            dz = (i + 1) % 4
            arrived(a2.at[dz], rs_r.at[dz, 2])
            tz[dz, low] = (
                part[dz, 0, 0, low].astype(F32) + a1[dz, 0].astype(F32) + a2[dz].astype(F32)
            ).astype(BF16)
            arrived(b2.at[dz], rs_r.at[dz, 3])
            tz[dz, high] = (
                part[dz, 0, 0, high].astype(F32) + b1[dz, 0].astype(F32) + b2[dz].astype(F32)
            ).astype(BF16)
            there = (4 - dz) % 4
            if self_too:
                send(tz.at[dz], landing.at[there], z_s.at[dz], r_sems.at[there], 1, zp(dz))
            else:
                @pl.when(dz != 0)
                def _():
                    send(tz.at[dz], landing.at[there], z_s.at[dz], r_sems.at[there], 1, zp(dz))

        each(0, 4, second)
        each(0, 4, third)

    def scatter_sent(self_too):
        def step(dz):
            sent(part.at[dz, pl.ds(0, 2), 1, low], rs_s.at[dz, 0])
            sent(part.at[dz, 1, pl.ds(0, 2), high], rs_s.at[dz, 1])
            sent(sa.at[dz], rs_s.at[dz, 2])
            sent(sb.at[dz], rs_s.at[dz, 3])

        each(0, 4, step)
        each(0 if self_too else 1, 4, lambda dz: sent(tz.at[dz], z_s.at[dz]))

    def scale_of(totals):
        return lax.rsqrt(totals[:, 0:1] / width + NORM_EPS)

    def set_normed(values, scale):
        normed = values.astype(F32) * scale
        nrm[...] = normed.astype(BF16)
        nrm_t[...] = jnp.transpose(normed).astype(BF16)

    @pl.when(sec == 0)
    def _():
        load_h.wait()
        entered = h0[...].astype(F32)
        stat_send(0, row_sums(entered * entered))
        load_w.wait()
        scatter_first(h0, 0, 4)
        load_c.wait()
        scatter_rest(zra, za_r, True)
        scale = scale_of(stat_total(0))
        set_normed(h0[...], scale)
        gather_rest(True)
        normed = nrm[...].astype(F32)
        stat_send(2, row_sums(back[...] * normed))
        gu[...] = gf[0, 0, 0, high]
        arrived(ad, ex_r.at[0])
        scatter_sent(True)
        stat_sent(0)
        rest_sent()
        dot = stat_total(2)[:, 0:1]
        own[...] = (
            gf[0, 0, 0].astype(F32) + scale * (back[...] - normed * dot / width)
        ).astype(BF16)
        send(own.at[high], gu, ex_s.at[0], ex_r.at[1], 1, dp)
        gd[...] = own[low]
        arrived(au, ex_r.at[2])
        stat_sent(2)
        sent(own.at[high], ex_s.at[0])

    @pl.when(sec == 1)
    def _():
        load_c.wait()
        gather_own(cot, 1, False)
        gf[0, 0, 0] = cot[...]
        load_h.wait()
        entered = h0[...].astype(F32)
        stat_send(0, row_sums(entered * entered))
        load_w.wait()
        gather_rest(False)
        scale = scale_of(stat_total(0))
        each(0, 4, lambda dz: arrived(zra.at[dz], za_r.at[dz]))
        mixed = (
            zra[0].astype(F32) + zra[1].astype(F32) + zra[2].astype(F32) + zra[3].astype(F32)
        )
        hid[...] = (h0[...].astype(F32) + scale * mixed).astype(BF16)
        hidden = hid[...].astype(F32)
        first = lax.broadcasted_iota(jnp.int32, (8, tok), 0) == 0
        stat_send(1, jnp.where(first, row_sums(hidden * hidden), row_sums(back[...] * hidden)))
        scatter_first(hid, 0, EARLY)
        own_sent(cot, False)
        totals = stat_total(1)
        scale = scale_of(totals)
        dot = totals[:, 1:2] * scale
        set_normed(hid[...], scale)
        own[...] = (
            cot[...].astype(F32) + scale * (back[...] - nrm[...].astype(F32) * dot / width)
        ).astype(BF16)
        gather_own(own, 0, True)
        scatter_first(hid, EARLY, 4)
        send(hid.at[low], ad, ex_s.at[0], ex_r.at[0], 0, dp)
        au[...] = hid[high]
        gd[...] = own[low]
        stat_sent(0)
        rest_sent()
        scatter_rest(zrb, zb_r, False)
        mixed = tz[0].astype(F32)
        for dz in (1, 2, 3):
            arrived(zrb.at[dz], zb_r.at[dz])
            mixed = mixed + zrb[dz].astype(F32)
        tz[0] = (hid[...].astype(F32) + scale * mixed).astype(BF16)
        send(tz.at[0, high], au, ex_s.at[1], ex_r.at[2], 0, dp)
        ad[...] = tz[0, low]
        own_sent(own, True)
        scatter_sent(False)
        stat_sent(1)
        sent(hid.at[low], ex_s.at[0])
        sent(tz.at[0, high], ex_s.at[1])
        arrived(gu, ex_r.at[1])


def finish_kernel(nrm_hbm, gf_hbm, *refs):
    held, outs = refs[:4], refs[4:8]
    wg_hbm, nrm_t, gf, wg, in_sem, wg_sem, out_sem = refs[8:]
    cols = nrm_t.shape[0]
    dp = lax.axis_index("dp")

    def load(k):
        return pltpu.make_async_copy(gf_hbm.at[k // 4, (k // 2) % 2, k % 2], gf.at[k], in_sem.at[k])

    def write(k):
        spot = peer_block(dp, k // 4, (k // 2) % 2, k % 2) * cols
        return pltpu.make_async_copy(
            wg.at[k], wg_hbm.at[:, pl.ds(pl.multiple_of(spot, cols), cols)], wg_sem.at[k])

    load_n = pltpu.make_async_copy(nrm_hbm, nrm_t, out_sem.at[4])
    load_n.start()
    each(0, 16, lambda k: load(k).start())
    copies = [pltpu.make_async_copy(held[k], outs[k], out_sem.at[k]) for k in range(4)]
    for copy in copies:
        copy.start()
    load_n.wait()

    def step(k):
        load(k).wait()
        wg[k] = jnp.dot(nrm_t[...], gf[k], preferred_element_type=F32)
        write(k).start()

    each(0, 16, step)
    for copy in copies:
        copy.wait()
    each(0, 16, lambda k: write(k).wait())


def direct_body(entering, cotangent, weights):
    streams, micro, tok_mb, cols = entering.shape
    tok = streams * micro * tok_mb
    half = tok // 2
    width = weights.shape[2]
    rows = entering.reshape(tok, cols)
    slopes = cotangent.reshape(tok, cols)
    vm = pl.BlockSpec(memory_space=pltpu.VMEM)
    hbm = pl.BlockSpec(memory_space=pl.ANY)
    half_out = jax.ShapeDtypeStruct((half, cols), BF16)
    dma = pltpu.SemaphoreType.DMA
    *kept, nrm_t, gathered = pl.pallas_call(
        window_kernel,
        out_shape=(half_out,) * 4 + (
            jax.ShapeDtypeStruct((cols, tok), BF16),
            jax.ShapeDtypeStruct((4, 2, 2, tok, cols), BF16),
        ),
        in_specs=[hbm, hbm, hbm],
        out_specs=(vm,) * 5 + (hbm,),
        scratch_shapes=[
            pltpu.VMEM((tok, cols), BF16),
            pltpu.VMEM((tok, cols), BF16),
            pltpu.VMEM((cols, width), BF16),
            pltpu.VMEM((4, 2, 2, tok, cols), BF16),
            pltpu.VMEM((4, 2, 2, tok, cols), BF16),
            pltpu.VMEM((4, 2, half, cols), BF16),
            pltpu.VMEM((4, 2, half, cols), BF16),
            pltpu.VMEM((4, half, cols), BF16),
            pltpu.VMEM((4, half, cols), BF16),
            pltpu.VMEM((4, half, cols), BF16),
            pltpu.VMEM((4, half, cols), BF16),
            pltpu.VMEM((4, tok, cols), BF16),
            pltpu.VMEM((4, tok, cols), BF16),
            pltpu.VMEM((4, tok, cols), BF16),
            pltpu.VMEM((3, 16, 2, tok), F32),
            pltpu.VMEM((tok, cols), F32),
            pltpu.VMEM((tok, cols), BF16),
            pltpu.VMEM((tok, cols), BF16),
            pltpu.VMEM((tok, cols), BF16),
            dma((3,)), dma((16,)), dma((3, 16)), dma((3, 16)),
            dma((4, 4)), dma((4, 5)), dma((6,)),
            dma((4, 4)), dma((4, 4)), dma((4,)), dma((4,)), dma((4,)),
            dma((2,)), dma((3,)),
        ],
        compiler_params=pltpu.CompilerParams(
            collective_id=0, has_side_effects=True, vmem_limit_bytes=63 * 1024 * 1024
        ),
        cost_estimate=pl.CostEstimate(
            flops=4 * tok * cols * width, bytes_accessed=4 * cols * width, transcendentals=2 * tok
        ),
    )(rows, slopes, weights)
    *outs, weight_grad = pl.pallas_call(
        finish_kernel,
        out_shape=(half_out,) * 4 + (jax.ShapeDtypeStruct((cols, width), F32),),
        in_specs=[hbm] * 6,
        out_specs=(hbm,) * 5,
        scratch_shapes=[
            pltpu.VMEM((cols, tok), BF16),
            pltpu.VMEM((16, tok, cols), BF16),
            pltpu.VMEM((16, cols, cols), F32),
            dma((16,)), dma((16,)), dma((5,)),
        ],
        compiler_params=pltpu.CompilerParams(vmem_limit_bytes=63 * 1024 * 1024),
        cost_estimate=pl.CostEstimate(
            flops=2 * tok * cols * width, bytes_accessed=6 * cols * width, transcendentals=0
        ),
    )(nrm_t, gathered, *kept)
    shape = (1, micro, tok_mb, cols)
    return (*(out.reshape(shape) for out in outs), weight_grad[None])


def solution(mesh):
    placed = (P(None, None, None, "dp"), P(None, None, None, "dp"), P("section", "dp", None))
    exact = dict(mesh.shape) == {"section": 2, "dp": 16}
    return jax.shard_map(
        direct_body if exact else body,
        mesh=mesh,
        in_specs=placed,
        out_specs=(
            P("section", None, None, "dp"),
            P("section", None, None, "dp"),
            P("section", None, None, "dp"),
            P("section", None, None, "dp"),
            P("section", "dp", None),
        ),
        check_vma=False,
    )
```

```python
import jax
import jax.numpy as jnp
from jax import lax
from jax.experimental import pallas as pl
from jax.experimental.pallas import tpu as pltpu
from jax.sharding import PartitionSpec as P

NORM_EPS = 1e-05


def for_sending(value):

    def short(part):
        return part.astype(jnp.bfloat16) if part.dtype == jnp.float32 else part

    return jax.tree.map(short, value)


def from_behind(value, axis, steps):
    count = lax.axis_size(axis)
    first, last = (max(0, -steps), min(count, count - steps))
    return lax.ppermute(value, axis, [(source, source + steps) for source in range(first, last)])


def swapped_2(block, axis, apart):
    count = lax.axis_size(axis)
    route = []
    for low in range(count):
        high = low | 1 << apart
        if high != low and high < count:
            route += [(low, high), (high, low)]
    return lax.ppermute(block, axis, route)


def pass_along(payload, ahead):
    if ahead:
        return jax.tree.map(
            lambda part, own: part.astype(own.dtype),
            from_behind(for_sending(payload), "section", 1),
            payload,
        )
    return jax.tree.map(
        lambda part, own: part.astype(own.dtype),
        from_behind(for_sending(payload), "section", -1),
        payload,
    )


def send_pair(down_part, up_part, down_ahead):
    return jnp.stack([pass_along(down_part, down_ahead), pass_along(up_part, not down_ahead)])


def section_bits():
    return lax.axis_size("section").bit_length() - 1


def mirror_weights(payload):
    for bit_idx in range(section_bits()):
        payload = swapped_2(payload, "section", bit_idx)
    return payload


def mirror_grads(payload):
    for bit_idx in range(section_bits()):
        payload = swapped_2(payload.astype(jnp.bfloat16), "section", bit_idx).astype(payload.dtype)
    return payload


def row_totals(first_part, second_part):
    return lax.psum((first_part, second_part), "dp")


def place_slot(store, stream, slot_idx, payload, is_live):
    previous = lax.dynamic_index_in_dim(store[stream], slot_idx, 0, keepdims=False)
    kept = jnp.where(is_live, payload.astype(store.dtype), previous)
    zero_idx = jnp.zeros((), jnp.int32)
    starts = (jnp.int32(stream), slot_idx) + (zero_idx,) * (store.ndim - 2)
    return lax.dynamic_update_slice(store, kept[None, None], starts)


def forward_cols(full_rows, input_cols, weight_cols):
    values = full_rows.astype(jnp.float32)
    row_scale = lax.rsqrt(jnp.mean(values * values, axis=1, keepdims=True) + NORM_EPS)
    normed = (values * row_scale).astype(jnp.bfloat16)
    mixed_cols = jnp.dot(normed, weight_cols, preferred_element_type=jnp.float32)
    output_cols = (input_cols.astype(jnp.float32) + mixed_cols).astype(jnp.bfloat16)
    return (output_cols, normed, mixed_cols, row_scale[:, 0])


def body(entering, cotangent, weights):
    section_count = lax.axis_size("section")
    last_section = section_count - 1
    section_idx = lax.axis_index("section")
    group_count = lax.axis_size("dp")
    local_cols = weights.shape[1]
    model_width = weights.shape[2]
    col_start = lax.axis_index("dp") * local_cols
    micro_count = entering.shape[1]
    tok_rows = entering.shape[2]
    tick_count = micro_count + section_count - 1
    own_rows = weights[0]
    held_rows = jnp.stack([own_rows, mirror_weights(own_rows)])
    up_delay = last_section - section_idx
    held_count = held_rows.shape[0]
    split_rows = held_rows.reshape(held_count, local_cols, group_count, local_cols)
    swapped = lax.all_to_all(split_rows, "dp", split_axis=2, concat_axis=1, tiled=True)
    held_cols = swapped.reshape(held_count, model_width, local_cols)
    held_last = held_count - 1
    fwd_delays = (section_idx, up_delay)
    back_delays = (last_section - section_idx, last_section - up_delay)

    def slot_of(tick_idx, delay_now):
        micro_idx = tick_idx - delay_now
        slot_idx = jnp.clip(micro_idx, 0, micro_count - 1)
        is_live = (micro_idx >= 0) & (micro_idx < micro_count)
        return (slot_idx, is_live)

    def forward_tick(tick_idx, state_now):
        inbox, normed_store, mixed_store, scale_store, act_store = state_now
        inputs_now = []
        slots_now = []
        for stream in range(2):
            slot_idx, is_live = slot_of(tick_idx, fwd_delays[stream])
            fresh = lax.dynamic_index_in_dim(entering[stream], slot_idx, 0, keepdims=False)
            inputs_now.append(jnp.where(fwd_delays[stream] == 0, fresh, inbox[stream]))
            slots_now.append((slot_idx, is_live))
        full_down, full_up = (
            lax.all_gather(for_sending(inputs_now[0]), "dp", axis=1, tiled=True),
            lax.all_gather(for_sending(inputs_now[1]), "dp", axis=1, tiled=True),
        )
        outputs_now = []
        for stream, full_rows in enumerate((full_down, full_up)):
            output_cols, normed, mixed_cols, row_scale = forward_cols(
                full_rows, inputs_now[stream], held_cols[stream * held_last]
            )
            slot_idx, is_live = slots_now[stream]
            normed_store = place_slot(normed_store, stream, slot_idx, normed, is_live)
            mixed_store = place_slot(mixed_store, stream, slot_idx, mixed_cols, is_live)
            scale_store = place_slot(scale_store, stream, slot_idx, row_scale, is_live)
            act_store = place_slot(act_store, stream, slot_idx, output_cols, is_live)
            outputs_now.append(output_cols)
        inbox = send_pair(outputs_now[0], outputs_now[1], True)
        return (inbox, normed_store, mixed_store, scale_store, act_store)

    start_fwd = (
        jnp.zeros((2, tok_rows, local_cols), jnp.bfloat16),
        jnp.zeros((2, micro_count, tok_rows, model_width), jnp.bfloat16),
        jnp.zeros((2, micro_count, tok_rows, local_cols), jnp.float32),
        jnp.zeros((2, micro_count, tok_rows), jnp.float32),
        jnp.zeros((2, micro_count, tok_rows, local_cols), jnp.bfloat16),
    )
    ended_fwd = lax.fori_loop(0, tick_count, forward_tick, start_fwd)
    normed_store, mixed_store, scale_store, act_store = (
        ended_fwd[1],
        ended_fwd[2],
        ended_fwd[3],
        ended_fwd[4],
    )

    def backward_tick(tick_idx, state_now):
        inbox, grad_store, weight_acc = state_now
        slopes_now = []
        picks = []
        for stream in range(2):
            slot_idx, is_live = slot_of(tick_idx, back_delays[stream])
            fresh = lax.dynamic_index_in_dim(cotangent[stream], slot_idx, 0, keepdims=False)
            slopes_now.append(jnp.where(back_delays[stream] == 0, fresh, inbox[stream]))
            normed = lax.dynamic_index_in_dim(normed_store[stream], slot_idx, 0, keepdims=False)
            mixed_cols = lax.dynamic_index_in_dim(mixed_store[stream], slot_idx, 0, keepdims=False)
            row_scale = lax.dynamic_index_in_dim(scale_store[stream], slot_idx, 0, keepdims=False)
            picks.append((slot_idx, is_live, normed, mixed_cols, row_scale))
        slope_down, slope_up = (
            lax.all_gather(for_sending(slopes_now[0]), "dp", axis=1, tiled=True),
            lax.all_gather(for_sending(slopes_now[1]), "dp", axis=1, tiled=True),
        )
        slope_fulls = (slope_down, slope_up)
        back_sums = []
        normed_locals = []
        for stream in range(2):
            back_sums.append(
                lax.dot_general(
                    slope_fulls[stream],
                    held_rows[stream * held_last],
                    (((1,), (1,)), ((), ())),
                    preferred_element_type=jnp.float32,
                )
            )
            normed_locals.append(
                lax.dynamic_slice_in_dim(picks[stream][2], col_start, local_cols, 1)
            )
        row_sums = row_totals(
            jnp.sum(back_sums[0] * normed_locals[0].astype(jnp.float32), axis=1),
            jnp.sum(back_sums[1] * normed_locals[1].astype(jnp.float32), axis=1),
        )
        grads_now = []
        for stream in range(2):
            slot_idx, is_live, normed, mixed_cols, row_scale = picks[stream]
            row_dot = row_sums[stream][:, None]
            normed_part = normed_locals[stream].astype(jnp.float32)
            grad_cols = (
                slopes_now[stream].astype(jnp.float32)
                + row_scale[:, None] * (back_sums[stream] - normed_part * row_dot / model_width)
            ).astype(jnp.bfloat16)
            weight_step = lax.dot_general(
                normed_locals[stream],
                slope_fulls[stream],
                (((0,), (0,)), ((), ())),
                preferred_element_type=jnp.float32,
            )
            weight_acc = weight_acc.at[stream].add(weight_step * is_live.astype(jnp.float32))
            grad_store = place_slot(grad_store, stream, slot_idx, grad_cols, is_live)
            grads_now.append(grad_cols)
        inbox = send_pair(grads_now[0], grads_now[1], False)
        return (inbox, grad_store, weight_acc)

    start_back = (
        jnp.zeros((2, tok_rows, local_cols), jnp.bfloat16),
        jnp.zeros((2, micro_count, tok_rows, local_cols), jnp.bfloat16),
        jnp.zeros((2, local_cols, model_width), jnp.float32),
    )
    ended_back = lax.fori_loop(0, tick_count, backward_tick, start_back)
    grad_store, weight_acc = (ended_back[1], ended_back[2])
    total_grad = weight_acc[0] + mirror_grads(weight_acc[1])
    acts_up = act_store[1]
    grads_up = grad_store[1]
    return (
        act_store[0][None],
        acts_up[None],
        grad_store[0][None],
        grads_up[None],
        total_grad[None],
    )


MESH = pl.DeviceIdType.MESH
F32 = jnp.float32
BF16 = jnp.bfloat16
EARLY = 2


def row_sums(values):
    ones = jnp.ones((8, values.shape[1]), F32)
    return lax.dot_general(
        ones,
        values,
        (((1,), (1,)), ((), ())),
        precision=lax.Precision.HIGHEST,
        preferred_element_type=F32,
    )


def peer_block(dp, dz, ry, rx):
    z, y, x = dp // 4, (dp // 2) % 2, dp % 2
    return ((z + dz) % 4) * 4 + ((y + ry) % 2) * 2 + (x + rx) % 2


def each(low, high, step):
    lax.fori_loop(low, high, lambda i, carry: (step(i), carry)[1], 0)


def window_kernel(
    h0_hbm, cot_hbm, w_hbm, ad, au, gd, gu, nrm_t, gf_hbm,
    h0, cot, w, gf, part, a1, b1, a2, b2, sa, sb, tz, zra, zrb, stats, back, hid, nrm, own, grown,
    early, e_s, e_r, in_sem, keep_sem, st_s, st_r, ag_s, ag_r, own_s, rs_s, rs_r, z_s, za_r, zb_r, ex_s, ex_r,
):
    tok, cols = h0.shape
    half = tok // 2
    low, high = pl.ds(0, half), pl.ds(half, half)
    width = cols * 16
    sec = lax.axis_index("section")
    dp = lax.axis_index("dp")
    px, py = peer_block(dp, 0, 0, 1), peer_block(dp, 0, 1, 0)

    def zp(dz):
        return peer_block(dp, dz, 0, 0)

    def block_cols(dz, ry, rx):
        return pl.ds(pl.multiple_of(peer_block(dp, dz, ry, rx) * cols, cols), cols)

    def remote(src, dst, s_sem, r_sem, section, chip):
        return pltpu.make_async_remote_copy(
            src_ref=src, dst_ref=dst, send_sem=s_sem, recv_sem=r_sem,
            device_id=(section, chip), device_id_type=MESH,
        )

    def send(*args):
        remote(*args).start()

    def arrived(dst, r_sem):
        remote(dst, dst, r_sem, r_sem, sec, dp).wait_recv()

    def sent(src, s_sem):
        remote(src, src, s_sem, s_sem, sec, dp).wait_send()

    load_h = pltpu.make_async_copy(h0_hbm, h0, in_sem.at[0])
    load_h.start()
    load_c = pltpu.make_async_copy(cot_hbm, cot, in_sem.at[1])
    load_c.start()
    load_w = pltpu.make_async_copy(w_hbm.at[0], w, in_sem.at[2])
    load_w.start()

    barrier = pltpu.get_barrier_semaphore()

    def greet(section, chip):
        pl.semaphore_signal(barrier, inc=1, device_id=(section, chip), device_id_type=MESH)

    for chip in (px, py, zp(1), zp(2), zp(3)):
        greet(sec, chip)

    @pl.when(sec == 1)
    def _():
        for chip in (dp, zp(1), zp(2), zp(3)):
            greet(0, chip)

    pl.semaphore_wait(barrier, 9 - 4 * sec)

    def early_z(value):
        early[0] = value[0:2]
        for dz in (1, 2, 3):
            send(early.at[0], early.at[4 - dz], e_s.at[dz], e_r.at[4 - dz], sec, zp(dz))

    def early_y():
        for dz in (1, 2, 3):
            arrived(early.at[dz], e_r.at[dz])
        early[6] = early[0] + early[1] + early[2] + early[3]
        send(early.at[6], early.at[4], e_s.at[4], e_r.at[4], sec, py)

    def early_x():
        arrived(early.at[4], e_r.at[4])
        early[7] = early[6] + early[4]
        send(early.at[7], early.at[5], e_s.at[5], e_r.at[5], sec, px)

    def early_total():
        arrived(early.at[5], e_r.at[5])
        each(1, 6, lambda k: sent(early.at[0], e_s.at[k]))
        return columns(early[7] + early[5])

    def columns(total):
        return jnp.transpose(jnp.concatenate([total] * 4, axis=0))

    def stat_send(k, value):
        stats[k, dp] = value[0:2]
        each(1, 16, lambda step: send(
            stats.at[k, dp], stats.at[k, dp], st_s.at[k, step], st_r.at[k, step],
            sec, (dp + step) % 16,
        ))

    def stat_total(k):
        each(1, 16, lambda step: arrived(stats.at[k, (dp + 16 - step) % 16], st_r.at[k, step]))
        return columns(jnp.sum(stats[k], axis=0))

    def stat_sent(k):
        each(1, 16, lambda step: sent(stats.at[k, dp], st_s.at[k, step]))

    def gather_own(src, section, include_self):
        for dz in (1, 2, 3):
            send(src, gf.at[4 - dz, 0, 0], own_s.at[dz], ag_r.at[4 - dz, 0], section, zp(dz))
        send(src, gf.at[0, 0, 1], own_s.at[4], ag_r.at[0, 1], section, px)
        send(src, gf.at[0, 1, 0], own_s.at[5], ag_r.at[0, 2], section, py)
        if include_self:
            send(src, gf.at[0, 0, 0], own_s.at[0], ag_r.at[0, 0], section, dp)

    def own_sent(src, include_self):
        each(0 if include_self else 1, 6, lambda k: sent(src, own_s.at[k]))

    def kept(dz, ry, rx):
        return pltpu.make_async_copy(
            gf.at[dz, ry, rx], gf_hbm.at[dz, ry, rx], keep_sem.at[dz * 4 + ry * 2 + rx])

    def use(dz, ry, rx):
        kept(dz, ry, rx).start()
        back[...] += lax.dot_general(
            gf[dz, ry, rx], w[:, block_cols(dz, ry, rx)], (((1,), (1,)), ((), ())),
            preferred_element_type=F32,
        )

    def gather_rest(own_arrives, after_z=lambda: None, after_xy=lambda: None):
        back[...] = jnp.zeros_like(back)

        def along_z(i):
            dz = (i + 1) % 4

            @pl.when(dz != 0)
            def _():
                arrived(gf.at[dz, 0, 0], ag_r.at[dz, 0])
                send(gf.at[dz, 0, 0], gf.at[dz, 0, 1], ag_s.at[dz, 0], ag_r.at[dz, 1], sec, px)
                send(gf.at[dz, 0, 0], gf.at[dz, 1, 0], ag_s.at[dz, 1], ag_r.at[dz, 2], sec, py)

            if own_arrives:
                @pl.when(dz == 0)
                def _():
                    arrived(gf.at[0, 0, 0], ag_r.at[0, 0])

            use(dz, 0, 0)

        def across(dz):
            arrived(gf.at[dz, 0, 1], ag_r.at[dz, 1])
            send(gf.at[dz, 0, 1, low], gf.at[dz, 1, 1, low], ag_s.at[dz, 2], ag_r.at[dz, 3], sec, py)
            arrived(gf.at[dz, 1, 0], ag_r.at[dz, 2])
            send(gf.at[dz, 1, 0, high], gf.at[dz, 1, 1, high], ag_s.at[dz, 3], ag_r.at[dz, 4], sec, px)
            each(0, 2, lambda k: use(dz, k, 1 - k))

        def diagonal(dz):
            arrived(gf.at[dz, 1, 1, low], ag_r.at[dz, 3])
            arrived(gf.at[dz, 1, 1, high], ag_r.at[dz, 4])
            use(dz, 1, 1)

        each(0, 4, along_z)
        after_z()
        each(0, 4, across)
        after_xy()
        each(0, 4, diagonal)

    def rest_sent():
        def forwarded(dz):
            sent(gf.at[dz, 0, 0], ag_s.at[dz, 0])
            sent(gf.at[dz, 0, 0], ag_s.at[dz, 1])

        def halves(dz):
            sent(gf.at[dz, 0, 1, low], ag_s.at[dz, 2])
            sent(gf.at[dz, 1, 0, high], ag_s.at[dz, 3])

        each(1, 4, forwarded)
        each(0, 4, halves)
        each(0, 16, lambda k: kept(k // 4, (k // 2) % 2, k % 2).wait())

    def scatter_first(rows, start, stop):
        def step(k):
            dz, j = (k // 4 + 1) % 4, k % 4
            ry, rx = 1 - j % 2, 1 - j // 2
            part[dz, ry, rx] = jnp.dot(
                rows[...], w[:, block_cols(dz, ry, rx)], preferred_element_type=F32
            ).astype(BF16)

            @pl.when(j == 1)
            def _():
                send(part.at[dz, pl.ds(0, 2), 1, low], a1.at[dz], rs_s.at[dz, 0], rs_r.at[dz, 0], sec, px)

            @pl.when(j == 2)
            def _():
                send(part.at[dz, 1, pl.ds(0, 2), high], b1.at[dz], rs_s.at[dz, 1], rs_r.at[dz, 1], sec, py)

        each(4 * start, 4 * stop, step)

    def scatter_rest(landing, r_sems, self_too, between=lambda: None):
        def second(i):
            dz = (i + 1) % 4
            arrived(a1.at[dz], rs_r.at[dz, 0])
            sa[dz] = (part[dz, 1, 0, low].astype(F32) + a1[dz, 1].astype(F32)).astype(BF16)
            send(sa.at[dz], a2.at[dz], rs_s.at[dz, 2], rs_r.at[dz, 2], sec, py)
            arrived(b1.at[dz], rs_r.at[dz, 1])
            sb[dz] = (part[dz, 0, 1, high].astype(F32) + b1[dz, 1].astype(F32)).astype(BF16)
            send(sb.at[dz], b2.at[dz], rs_s.at[dz, 3], rs_r.at[dz, 3], sec, px)

        def third(i):
            dz = (i + 1) % 4
            arrived(a2.at[dz], rs_r.at[dz, 2])
            tz[dz, low] = (
                part[dz, 0, 0, low].astype(F32) + a1[dz, 0].astype(F32) + a2[dz].astype(F32)
            ).astype(BF16)
            arrived(b2.at[dz], rs_r.at[dz, 3])
            tz[dz, high] = (
                part[dz, 0, 0, high].astype(F32) + b1[dz, 0].astype(F32) + b2[dz].astype(F32)
            ).astype(BF16)
            there = (4 - dz) % 4
            if self_too:
                send(tz.at[dz], landing.at[there], z_s.at[dz], r_sems.at[there], 1, zp(dz))
            else:
                @pl.when(dz != 0)
                def _():
                    send(tz.at[dz], landing.at[there], z_s.at[dz], r_sems.at[there], 1, zp(dz))

        each(0, 4, second)
        between()
        each(0, 4, third)

    def scatter_sent(self_too):
        def step(dz):
            sent(part.at[dz, pl.ds(0, 2), 1, low], rs_s.at[dz, 0])
            sent(part.at[dz, 1, pl.ds(0, 2), high], rs_s.at[dz, 1])
            sent(sa.at[dz], rs_s.at[dz, 2])
            sent(sb.at[dz], rs_s.at[dz, 3])

        each(0, 4, step)
        each(0 if self_too else 1, 4, lambda dz: sent(tz.at[dz], z_s.at[dz]))

    def scale_of(totals):
        return lax.rsqrt(totals[:, 0:1] / width + NORM_EPS)

    def set_normed(values, scale):
        normed = values.astype(F32) * scale
        nrm[...] = normed.astype(BF16)
        nrm_t[...] = jnp.transpose(normed).astype(BF16)

    @pl.when(sec == 0)
    def _():
        load_h.wait()
        entered = h0[...].astype(F32)
        early_z(row_sums(entered * entered))
        load_w.wait()
        scatter_first(h0, 0, 4)
        load_c.wait()
        early_y()
        scatter_rest(zra, za_r, True, early_x)
        scale = scale_of(early_total())
        set_normed(h0[...], scale)
        gather_rest(True)
        normed = nrm[...].astype(F32)
        gu[...] = gf[0, 0, 0, high]
        arrived(ad, ex_r.at[0])
        scatter_sent(True)
        rest_sent()
        each(0, 16, lambda step: arrived(stats.at[1, (dp + 16 - step) % 16], st_r.at[1, step]))
        dot = columns(jnp.sum(stats[1], axis=0))[:, 0:1]
        own[...] = (
            gf[0, 0, 0].astype(F32) + scale * (back[...] - normed * dot / width)
        ).astype(BF16)
        send(own.at[high], gu, ex_s.at[0], ex_r.at[1], 1, dp)
        gd[...] = own[low]
        arrived(au, ex_r.at[2])
        sent(own.at[high], ex_s.at[0])

    @pl.when(sec == 1)
    def _():
        load_c.wait()
        gather_own(cot, 1, False)
        gf[0, 0, 0] = cot[...]
        load_h.wait()
        entered = h0[...].astype(F32)
        early_z(row_sums(entered * entered))
        load_w.wait()
        gather_rest(False, early_y, early_x)
        scale = scale_of(early_total())
        each(0, 4, lambda dz: arrived(zra.at[dz], za_r.at[dz]))
        mixed = (
            zra[0].astype(F32) + zra[1].astype(F32) + zra[2].astype(F32) + zra[3].astype(F32)
        )
        grown[...] = scale * mixed
        hid[...] = (h0[...].astype(F32) + grown[...]).astype(BF16)
        hidden = hid[...].astype(F32)
        first = lax.broadcasted_iota(jnp.int32, (8, tok), 0) == 0
        stat_send(0, jnp.where(first, row_sums(hidden * hidden), row_sums(back[...] * hidden)))
        scatter_first(hid, 0, EARLY)
        own_sent(cot, False)
        totals = stat_total(0)
        scale = scale_of(totals)
        dot = totals[:, 1:2] * scale
        set_normed(hid[...], scale)
        own[...] = (
            cot[...].astype(F32) + scale * (back[...] - nrm[...].astype(F32) * dot / width)
        ).astype(BF16)
        gather_own(own, 0, True)
        early[0] = row_sums(own[...].astype(F32) * grown[...])[0:2]
        each(0, 16, lambda step: send(
            early.at[0], stats.at[1, dp], st_s.at[1, step], st_r.at[1, step], 0, (dp + step) % 16))
        scatter_first(hid, EARLY, 4)
        send(hid.at[low], ad, ex_s.at[0], ex_r.at[0], 0, dp)
        au[...] = hid[high]
        gd[...] = own[low]
        rest_sent()
        scatter_rest(zrb, zb_r, False)
        mixed = tz[0].astype(F32)
        for dz in (1, 2, 3):
            arrived(zrb.at[dz], zb_r.at[dz])
            mixed = mixed + zrb[dz].astype(F32)
        tz[0] = (hid[...].astype(F32) + scale * mixed).astype(BF16)
        send(tz.at[0, high], au, ex_s.at[1], ex_r.at[2], 0, dp)
        ad[...] = tz[0, low]
        own_sent(own, True)
        scatter_sent(False)
        stat_sent(0)
        each(0, 16, lambda step: sent(early.at[0], st_s.at[1, step]))
        sent(hid.at[low], ex_s.at[0])
        sent(tz.at[0, high], ex_s.at[1])
        arrived(gu, ex_r.at[1])


def finish_kernel(nrm_hbm, gf_hbm, *refs):
    held, outs = refs[:4], refs[4:8]
    wg_hbm, nrm_t, gf, wg, small, in_sem, wg_sem, held_sem, out_sem = refs[8:]
    cols = nrm_t.shape[0]
    dp = lax.axis_index("dp")

    def load(k):
        return pltpu.make_async_copy(gf_hbm.at[k // 4, (k // 2) % 2, k % 2], gf.at[k], in_sem.at[k])

    def write(k):
        spot = peer_block(dp, k // 4, (k // 2) % 2, k % 2) * cols
        return pltpu.make_async_copy(
            wg.at[k], wg_hbm.at[:, pl.ds(pl.multiple_of(spot, cols), cols)], wg_sem.at[k])

    load_n = pltpu.make_async_copy(nrm_hbm, nrm_t, held_sem.at[4])
    load_n.start()
    each(0, 16, lambda k: load(k).start())
    takes = [pltpu.make_async_copy(held[k], small.at[k], held_sem.at[k]) for k in range(4)]
    copies = [pltpu.make_async_copy(small.at[k], outs[k], out_sem.at[k]) for k in range(4)]
    for copy in takes:
        copy.start()
    load_n.wait()

    def step(k):
        load(k).wait()
        wg[k] = jnp.dot(nrm_t[...], gf[k], preferred_element_type=F32)
        write(k).start()

    each(0, 16, step)
    for take, copy in zip(takes, copies):
        take.wait()
        copy.start()
    for copy in copies:
        copy.wait()
    each(0, 16, lambda k: write(k).wait())


def direct_body(entering, cotangent, weights):
    streams, micro, tok_mb, cols = entering.shape
    tok = streams * micro * tok_mb
    half = tok // 2
    width = weights.shape[2]
    rows = entering.reshape(tok, cols)
    slopes = cotangent.reshape(tok, cols)
    vm = pl.BlockSpec(memory_space=pltpu.VMEM)
    hbm = pl.BlockSpec(memory_space=pl.ANY)
    half_out = jax.ShapeDtypeStruct((half, cols), BF16)
    dma = pltpu.SemaphoreType.DMA
    *kept, nrm_t, gathered = pl.pallas_call(
        window_kernel,
        out_shape=(half_out,) * 4 + (
            jax.ShapeDtypeStruct((cols, tok), BF16),
            jax.ShapeDtypeStruct((4, 2, 2, tok, cols), BF16),
        ),
        in_specs=[hbm, hbm, hbm],
        out_specs=(vm,) * 5 + (hbm,),
        scratch_shapes=[
            pltpu.VMEM((tok, cols), BF16),
            pltpu.VMEM((tok, cols), BF16),
            pltpu.VMEM((cols, width), BF16),
            pltpu.VMEM((4, 2, 2, tok, cols), BF16),
            pltpu.VMEM((4, 2, 2, tok, cols), BF16),
            pltpu.VMEM((4, 2, half, cols), BF16),
            pltpu.VMEM((4, 2, half, cols), BF16),
            pltpu.VMEM((4, half, cols), BF16),
            pltpu.VMEM((4, half, cols), BF16),
            pltpu.VMEM((4, half, cols), BF16),
            pltpu.VMEM((4, half, cols), BF16),
            pltpu.VMEM((4, tok, cols), BF16),
            pltpu.VMEM((4, tok, cols), BF16),
            pltpu.VMEM((4, tok, cols), BF16),
            pltpu.VMEM((2, 16, 2, tok), F32),
            pltpu.VMEM((tok, cols), F32),
            pltpu.VMEM((tok, cols), BF16),
            pltpu.VMEM((tok, cols), BF16),
            pltpu.VMEM((tok, cols), BF16),
            pltpu.VMEM((tok, cols), F32),
            pltpu.VMEM((8, 2, tok), F32), dma((6,)), dma((6,)),
            dma((3,)), dma((16,)), dma((2, 16)), dma((2, 16)),
            dma((4, 4)), dma((4, 5)), dma((6,)),
            dma((4, 4)), dma((4, 4)), dma((4,)), dma((4,)), dma((4,)),
            dma((2,)), dma((3,)),
        ],
        compiler_params=pltpu.CompilerParams(
            collective_id=0, has_side_effects=True, vmem_limit_bytes=63 * 1024 * 1024
        ),
        cost_estimate=pl.CostEstimate(
            flops=4 * tok * cols * width, bytes_accessed=4 * cols * width, transcendentals=2 * tok
        ),
    )(rows, slopes, weights)
    *outs, weight_grad = pl.pallas_call(
        finish_kernel,
        out_shape=(half_out,) * 4 + (jax.ShapeDtypeStruct((cols, width), F32),),
        in_specs=[hbm] * 6,
        out_specs=(hbm,) * 5,
        scratch_shapes=[
            pltpu.VMEM((cols, tok), BF16),
            pltpu.VMEM((16, tok, cols), BF16),
            pltpu.VMEM((16, cols, cols), F32),
            pltpu.VMEM((4, half, cols), BF16),
            dma((16,)), dma((16,)), dma((5,)), dma((4,)),
        ],
        compiler_params=pltpu.CompilerParams(vmem_limit_bytes=63 * 1024 * 1024),
        cost_estimate=pl.CostEstimate(
            flops=2 * tok * cols * width, bytes_accessed=6 * cols * width, transcendentals=0
        ),
    )(nrm_t, gathered, *kept)
    shape = (1, micro, tok_mb, cols)
    return (*(out.reshape(shape) for out in outs), weight_grad[None])


def solution(mesh):
    placed = (P(None, None, None, "dp"), P(None, None, None, "dp"), P("section", "dp", None))
    exact = dict(mesh.shape) == {"section": 2, "dp": 16}
    return jax.shard_map(
        direct_body if exact else body,
        mesh=mesh,
        in_specs=placed,
        out_specs=(
            P("section", None, None, "dp"),
            P("section", None, None, "dp"),
            P("section", None, None, "dp"),
            P("section", None, None, "dp"),
            P("section", "dp", None),
        ),
        check_vma=False,
    )
```

```python
import jax
import jax.numpy as jnp
from jax import lax
from jax.experimental import pallas as pl
from jax.experimental.pallas import tpu as pltpu
from jax.sharding import PartitionSpec as P

NORM_EPS = 1e-05


def for_sending(value):

    def short(part):
        return part.astype(jnp.bfloat16) if part.dtype == jnp.float32 else part

    return jax.tree.map(short, value)


def from_behind(value, axis, steps):
    count = lax.axis_size(axis)
    first, last = (max(0, -steps), min(count, count - steps))
    return lax.ppermute(value, axis, [(source, source + steps) for source in range(first, last)])


def swapped_2(block, axis, apart):
    count = lax.axis_size(axis)
    route = []
    for low in range(count):
        high = low | 1 << apart
        if high != low and high < count:
            route += [(low, high), (high, low)]
    return lax.ppermute(block, axis, route)


def pass_along(payload, ahead):
    if ahead:
        return jax.tree.map(
            lambda part, own: part.astype(own.dtype),
            from_behind(for_sending(payload), "section", 1),
            payload,
        )
    return jax.tree.map(
        lambda part, own: part.astype(own.dtype),
        from_behind(for_sending(payload), "section", -1),
        payload,
    )


def send_pair(down_part, up_part, down_ahead):
    return jnp.stack([pass_along(down_part, down_ahead), pass_along(up_part, not down_ahead)])


def section_bits():
    return lax.axis_size("section").bit_length() - 1


def mirror_weights(payload):
    for bit_idx in range(section_bits()):
        payload = swapped_2(payload, "section", bit_idx)
    return payload


def mirror_grads(payload):
    for bit_idx in range(section_bits()):
        payload = swapped_2(payload.astype(jnp.bfloat16), "section", bit_idx).astype(payload.dtype)
    return payload


def row_totals(first_part, second_part):
    return lax.psum((first_part, second_part), "dp")


def place_slot(store, stream, slot_idx, payload, is_live):
    previous = lax.dynamic_index_in_dim(store[stream], slot_idx, 0, keepdims=False)
    kept = jnp.where(is_live, payload.astype(store.dtype), previous)
    zero_idx = jnp.zeros((), jnp.int32)
    starts = (jnp.int32(stream), slot_idx) + (zero_idx,) * (store.ndim - 2)
    return lax.dynamic_update_slice(store, kept[None, None], starts)


def forward_cols(full_rows, input_cols, weight_cols):
    values = full_rows.astype(jnp.float32)
    row_scale = lax.rsqrt(jnp.mean(values * values, axis=1, keepdims=True) + NORM_EPS)
    normed = (values * row_scale).astype(jnp.bfloat16)
    mixed_cols = jnp.dot(normed, weight_cols, preferred_element_type=jnp.float32)
    output_cols = (input_cols.astype(jnp.float32) + mixed_cols).astype(jnp.bfloat16)
    return (output_cols, normed, mixed_cols, row_scale[:, 0])


def body(entering, cotangent, weights):
    section_count = lax.axis_size("section")
    last_section = section_count - 1
    section_idx = lax.axis_index("section")
    group_count = lax.axis_size("dp")
    local_cols = weights.shape[1]
    model_width = weights.shape[2]
    col_start = lax.axis_index("dp") * local_cols
    micro_count = entering.shape[1]
    tok_rows = entering.shape[2]
    tick_count = micro_count + section_count - 1
    own_rows = weights[0]
    held_rows = jnp.stack([own_rows, mirror_weights(own_rows)])
    up_delay = last_section - section_idx
    held_count = held_rows.shape[0]
    split_rows = held_rows.reshape(held_count, local_cols, group_count, local_cols)
    swapped = lax.all_to_all(split_rows, "dp", split_axis=2, concat_axis=1, tiled=True)
    held_cols = swapped.reshape(held_count, model_width, local_cols)
    held_last = held_count - 1
    fwd_delays = (section_idx, up_delay)
    back_delays = (last_section - section_idx, last_section - up_delay)

    def slot_of(tick_idx, delay_now):
        micro_idx = tick_idx - delay_now
        slot_idx = jnp.clip(micro_idx, 0, micro_count - 1)
        is_live = (micro_idx >= 0) & (micro_idx < micro_count)
        return (slot_idx, is_live)

    def forward_tick(tick_idx, state_now):
        inbox, normed_store, mixed_store, scale_store, act_store = state_now
        inputs_now = []
        slots_now = []
        for stream in range(2):
            slot_idx, is_live = slot_of(tick_idx, fwd_delays[stream])
            fresh = lax.dynamic_index_in_dim(entering[stream], slot_idx, 0, keepdims=False)
            inputs_now.append(jnp.where(fwd_delays[stream] == 0, fresh, inbox[stream]))
            slots_now.append((slot_idx, is_live))
        full_down, full_up = (
            lax.all_gather(for_sending(inputs_now[0]), "dp", axis=1, tiled=True),
            lax.all_gather(for_sending(inputs_now[1]), "dp", axis=1, tiled=True),
        )
        outputs_now = []
        for stream, full_rows in enumerate((full_down, full_up)):
            output_cols, normed, mixed_cols, row_scale = forward_cols(
                full_rows, inputs_now[stream], held_cols[stream * held_last]
            )
            slot_idx, is_live = slots_now[stream]
            normed_store = place_slot(normed_store, stream, slot_idx, normed, is_live)
            mixed_store = place_slot(mixed_store, stream, slot_idx, mixed_cols, is_live)
            scale_store = place_slot(scale_store, stream, slot_idx, row_scale, is_live)
            act_store = place_slot(act_store, stream, slot_idx, output_cols, is_live)
            outputs_now.append(output_cols)
        inbox = send_pair(outputs_now[0], outputs_now[1], True)
        return (inbox, normed_store, mixed_store, scale_store, act_store)

    start_fwd = (
        jnp.zeros((2, tok_rows, local_cols), jnp.bfloat16),
        jnp.zeros((2, micro_count, tok_rows, model_width), jnp.bfloat16),
        jnp.zeros((2, micro_count, tok_rows, local_cols), jnp.float32),
        jnp.zeros((2, micro_count, tok_rows), jnp.float32),
        jnp.zeros((2, micro_count, tok_rows, local_cols), jnp.bfloat16),
    )
    ended_fwd = lax.fori_loop(0, tick_count, forward_tick, start_fwd)
    normed_store, mixed_store, scale_store, act_store = (
        ended_fwd[1],
        ended_fwd[2],
        ended_fwd[3],
        ended_fwd[4],
    )

    def backward_tick(tick_idx, state_now):
        inbox, grad_store, weight_acc = state_now
        slopes_now = []
        picks = []
        for stream in range(2):
            slot_idx, is_live = slot_of(tick_idx, back_delays[stream])
            fresh = lax.dynamic_index_in_dim(cotangent[stream], slot_idx, 0, keepdims=False)
            slopes_now.append(jnp.where(back_delays[stream] == 0, fresh, inbox[stream]))
            normed = lax.dynamic_index_in_dim(normed_store[stream], slot_idx, 0, keepdims=False)
            mixed_cols = lax.dynamic_index_in_dim(mixed_store[stream], slot_idx, 0, keepdims=False)
            row_scale = lax.dynamic_index_in_dim(scale_store[stream], slot_idx, 0, keepdims=False)
            picks.append((slot_idx, is_live, normed, mixed_cols, row_scale))
        slope_down, slope_up = (
            lax.all_gather(for_sending(slopes_now[0]), "dp", axis=1, tiled=True),
            lax.all_gather(for_sending(slopes_now[1]), "dp", axis=1, tiled=True),
        )
        slope_fulls = (slope_down, slope_up)
        back_sums = []
        normed_locals = []
        for stream in range(2):
            back_sums.append(
                lax.dot_general(
                    slope_fulls[stream],
                    held_rows[stream * held_last],
                    (((1,), (1,)), ((), ())),
                    preferred_element_type=jnp.float32,
                )
            )
            normed_locals.append(
                lax.dynamic_slice_in_dim(picks[stream][2], col_start, local_cols, 1)
            )
        row_sums = row_totals(
            jnp.sum(back_sums[0] * normed_locals[0].astype(jnp.float32), axis=1),
            jnp.sum(back_sums[1] * normed_locals[1].astype(jnp.float32), axis=1),
        )
        grads_now = []
        for stream in range(2):
            slot_idx, is_live, normed, mixed_cols, row_scale = picks[stream]
            row_dot = row_sums[stream][:, None]
            normed_part = normed_locals[stream].astype(jnp.float32)
            grad_cols = (
                slopes_now[stream].astype(jnp.float32)
                + row_scale[:, None] * (back_sums[stream] - normed_part * row_dot / model_width)
            ).astype(jnp.bfloat16)
            weight_step = lax.dot_general(
                normed_locals[stream],
                slope_fulls[stream],
                (((0,), (0,)), ((), ())),
                preferred_element_type=jnp.float32,
            )
            weight_acc = weight_acc.at[stream].add(weight_step * is_live.astype(jnp.float32))
            grad_store = place_slot(grad_store, stream, slot_idx, grad_cols, is_live)
            grads_now.append(grad_cols)
        inbox = send_pair(grads_now[0], grads_now[1], False)
        return (inbox, grad_store, weight_acc)

    start_back = (
        jnp.zeros((2, tok_rows, local_cols), jnp.bfloat16),
        jnp.zeros((2, micro_count, tok_rows, local_cols), jnp.bfloat16),
        jnp.zeros((2, local_cols, model_width), jnp.float32),
    )
    ended_back = lax.fori_loop(0, tick_count, backward_tick, start_back)
    grad_store, weight_acc = (ended_back[1], ended_back[2])
    total_grad = weight_acc[0] + mirror_grads(weight_acc[1])
    acts_up = act_store[1]
    grads_up = grad_store[1]
    return (
        act_store[0][None],
        acts_up[None],
        grad_store[0][None],
        grads_up[None],
        total_grad[None],
    )


MESH = pl.DeviceIdType.MESH
F32 = jnp.float32
BF16 = jnp.bfloat16


def row_sums(values):
    ones = jnp.ones((8, values.shape[1]), F32)
    return lax.dot_general(
        ones,
        values,
        (((1,), (1,)), ((), ())),
        precision=lax.Precision.HIGHEST,
        preferred_element_type=F32,
    )


def peer_block(dp, dz, ry, rx):
    z, y, x = dp // 4, (dp // 2) % 2, dp % 2
    return ((z + dz) % 4) * 4 + ((y + ry) % 2) * 2 + (x + rx) % 2


def each(low, high, step):
    lax.fori_loop(low, high, lambda i, carry: (step(i), carry)[1], 0)


def window_kernel(
    h0_hbm, cot_hbm, w_hbm, ad, au, gd, gu, nrm_t, gf_hbm,
    h0, cot, w, gf, part, a1, b1, a2, b2, sa, sb, tz, zra, zrb, stats, back, hid, nrm, own, grown,
    early, e_s, e_r, in_sem, keep_sem, st_s, st_r, ag_s, ag_r, own_s, rs_s, rs_r, z_s, za_r, zb_r, ex_s, ex_r,
):
    tok, cols = h0.shape
    half = tok // 2
    low, high = pl.ds(0, half), pl.ds(half, half)
    width = cols * 16
    sec = lax.axis_index("section")
    dp = lax.axis_index("dp")
    px, py = peer_block(dp, 0, 0, 1), peer_block(dp, 0, 1, 0)

    def zp(dz):
        return peer_block(dp, dz, 0, 0)

    def block_cols(dz, ry, rx):
        return pl.ds(pl.multiple_of(peer_block(dp, dz, ry, rx) * cols, cols), cols)

    def remote(src, dst, s_sem, r_sem, section, chip):
        return pltpu.make_async_remote_copy(
            src_ref=src, dst_ref=dst, send_sem=s_sem, recv_sem=r_sem,
            device_id=(section, chip), device_id_type=MESH,
        )

    def send(*args):
        remote(*args).start()

    def arrived(dst, r_sem):
        remote(dst, dst, r_sem, r_sem, sec, dp).wait_recv()

    def sent(src, s_sem):
        remote(src, src, s_sem, s_sem, sec, dp).wait_send()

    load_h = pltpu.make_async_copy(h0_hbm, h0, in_sem.at[0])
    load_h.start()
    load_c = pltpu.make_async_copy(cot_hbm, cot, in_sem.at[1])
    load_c.start()
    load_w = pltpu.make_async_copy(w_hbm.at[0], w, in_sem.at[2])
    load_w.start()

    barrier = pltpu.get_barrier_semaphore()

    def greet(section, chip):
        pl.semaphore_signal(barrier, inc=1, device_id=(section, chip), device_id_type=MESH)

    for chip in (px, py, zp(1), zp(2), zp(3)):
        greet(sec, chip)

    @pl.when(sec == 1)
    def _():
        for chip in (dp, zp(1), zp(2), zp(3)):
            greet(0, chip)

    pl.semaphore_wait(barrier, 9 - 4 * sec)

    def early_z(value):
        early[0] = value[0:2]
        for dz in (1, 2, 3):
            send(early.at[0], early.at[4 - dz], e_s.at[dz], e_r.at[4 - dz], sec, zp(dz))

    def early_y():
        for dz in (1, 2, 3):
            arrived(early.at[dz], e_r.at[dz])
        early[6] = early[0] + early[1] + early[2] + early[3]
        send(early.at[6], early.at[4], e_s.at[4], e_r.at[4], sec, py)

    def early_x():
        arrived(early.at[4], e_r.at[4])
        early[7] = early[6] + early[4]
        send(early.at[7], early.at[5], e_s.at[5], e_r.at[5], sec, px)

    def early_total():
        arrived(early.at[5], e_r.at[5])
        each(1, 6, lambda k: sent(early.at[0], e_s.at[k]))
        return columns(early[7] + early[5])

    def columns(total):
        return jnp.transpose(jnp.concatenate([total] * 4, axis=0))

    def stat_send(k, value):
        stats[k, dp] = value[0:2]
        each(1, 16, lambda step: send(
            stats.at[k, dp], stats.at[k, dp], st_s.at[k, step], st_r.at[k, step],
            sec, (dp + step) % 16,
        ))

    def stat_total(k):
        each(1, 16, lambda step: arrived(stats.at[k, (dp + 16 - step) % 16], st_r.at[k, step]))
        return columns(jnp.sum(stats[k], axis=0))

    def stat_sent(k):
        each(1, 16, lambda step: sent(stats.at[k, dp], st_s.at[k, step]))

    def gather_own(src, section, include_self):
        for dz in (1, 2, 3):
            send(src, gf.at[4 - dz, 0, 0], own_s.at[dz], ag_r.at[4 - dz, 0], section, zp(dz))
        send(src, gf.at[0, 0, 1], own_s.at[4], ag_r.at[0, 1], section, px)
        send(src, gf.at[0, 1, 0], own_s.at[5], ag_r.at[0, 2], section, py)
        if include_self:
            send(src, gf.at[0, 0, 0], own_s.at[0], ag_r.at[0, 0], section, dp)

    def own_sent(src, include_self):
        each(0 if include_self else 1, 6, lambda k: sent(src, own_s.at[k]))

    def kept(dz, ry, rx):
        return pltpu.make_async_copy(
            gf.at[dz, ry, rx], gf_hbm.at[dz, ry, rx], keep_sem.at[dz * 4 + ry * 2 + rx])

    def use(dz, ry, rx):
        kept(dz, ry, rx).start()
        back[...] += lax.dot_general(
            gf[dz, ry, rx], w[:, block_cols(dz, ry, rx)], (((1,), (1,)), ((), ())),
            preferred_element_type=F32,
        )

    def gather_rest(own_arrives, after_z=lambda: None, after_xy=lambda: None):
        back[...] = jnp.zeros_like(back)

        def along_z(i):
            dz = (i + 1) % 4

            @pl.when(dz != 0)
            def _():
                arrived(gf.at[dz, 0, 0], ag_r.at[dz, 0])
                send(gf.at[dz, 0, 0], gf.at[dz, 0, 1], ag_s.at[dz, 0], ag_r.at[dz, 1], sec, px)
                send(gf.at[dz, 0, 0], gf.at[dz, 1, 0], ag_s.at[dz, 1], ag_r.at[dz, 2], sec, py)

            if own_arrives:
                @pl.when(dz == 0)
                def _():
                    arrived(gf.at[0, 0, 0], ag_r.at[0, 0])

            use(dz, 0, 0)

        def across(dz):
            arrived(gf.at[dz, 0, 1], ag_r.at[dz, 1])
            send(gf.at[dz, 0, 1, low], gf.at[dz, 1, 1, low], ag_s.at[dz, 2], ag_r.at[dz, 3], sec, py)
            arrived(gf.at[dz, 1, 0], ag_r.at[dz, 2])
            send(gf.at[dz, 1, 0, high], gf.at[dz, 1, 1, high], ag_s.at[dz, 3], ag_r.at[dz, 4], sec, px)
            each(0, 2, lambda k: use(dz, k, 1 - k))

        def diagonal(dz):
            arrived(gf.at[dz, 1, 1, low], ag_r.at[dz, 3])
            arrived(gf.at[dz, 1, 1, high], ag_r.at[dz, 4])
            use(dz, 1, 1)

        each(0, 4, along_z)
        after_z()
        each(0, 4, across)
        after_xy()
        each(0, 4, diagonal)

    def rest_sent():
        def forwarded(dz):
            sent(gf.at[dz, 0, 0], ag_s.at[dz, 0])
            sent(gf.at[dz, 0, 0], ag_s.at[dz, 1])

        def halves(dz):
            sent(gf.at[dz, 0, 1, low], ag_s.at[dz, 2])
            sent(gf.at[dz, 1, 0, high], ag_s.at[dz, 3])

        each(1, 4, forwarded)
        each(0, 4, halves)
        each(0, 16, lambda k: kept(k // 4, (k // 2) % 2, k % 2).wait())

    def scatter_first(rows, start, stop):
        def step(k):
            dz, j = (k // 4 + 1) % 4, k % 4
            ry, rx = 1 - j % 2, 1 - j // 2
            part[dz, ry, rx] = jnp.dot(
                rows[...], w[:, block_cols(dz, ry, rx)], preferred_element_type=F32
            ).astype(BF16)

            @pl.when(j == 1)
            def _():
                send(part.at[dz, pl.ds(0, 2), 1, low], a1.at[dz], rs_s.at[dz, 0], rs_r.at[dz, 0], sec, px)

            @pl.when(j == 2)
            def _():
                send(part.at[dz, 1, pl.ds(0, 2), high], b1.at[dz], rs_s.at[dz, 1], rs_r.at[dz, 1], sec, py)

        each(4 * start, 4 * stop, step)

    def scatter_rest(landing, r_sems, self_too, between=lambda: None):
        def second(i):
            dz = (i + 1) % 4
            arrived(a1.at[dz], rs_r.at[dz, 0])
            sa[dz] = (part[dz, 1, 0, low].astype(F32) + a1[dz, 1].astype(F32)).astype(BF16)
            send(sa.at[dz], a2.at[dz], rs_s.at[dz, 2], rs_r.at[dz, 2], sec, py)
            arrived(b1.at[dz], rs_r.at[dz, 1])
            sb[dz] = (part[dz, 0, 1, high].astype(F32) + b1[dz, 1].astype(F32)).astype(BF16)
            send(sb.at[dz], b2.at[dz], rs_s.at[dz, 3], rs_r.at[dz, 3], sec, px)

        def third(i):
            dz = (i + 1) % 4
            arrived(a2.at[dz], rs_r.at[dz, 2])
            tz[dz, low] = (
                part[dz, 0, 0, low].astype(F32) + a1[dz, 0].astype(F32) + a2[dz].astype(F32)
            ).astype(BF16)
            arrived(b2.at[dz], rs_r.at[dz, 3])
            tz[dz, high] = (
                part[dz, 0, 0, high].astype(F32) + b1[dz, 0].astype(F32) + b2[dz].astype(F32)
            ).astype(BF16)
            there = (4 - dz) % 4
            if self_too:
                send(tz.at[dz], landing.at[there], z_s.at[dz], r_sems.at[there], 1, zp(dz))
            else:
                @pl.when(dz != 0)
                def _():
                    send(tz.at[dz], landing.at[there], z_s.at[dz], r_sems.at[there], 1, zp(dz))

        each(0, 4, second)
        between()
        each(0, 4, third)

    def scatter_sent(self_too):
        def step(dz):
            sent(part.at[dz, pl.ds(0, 2), 1, low], rs_s.at[dz, 0])
            sent(part.at[dz, 1, pl.ds(0, 2), high], rs_s.at[dz, 1])
            sent(sa.at[dz], rs_s.at[dz, 2])
            sent(sb.at[dz], rs_s.at[dz, 3])

        each(0, 4, step)
        each(0 if self_too else 1, 4, lambda dz: sent(tz.at[dz], z_s.at[dz]))

    def scale_of(totals):
        return lax.rsqrt(totals[:, 0:1] / width + NORM_EPS)

    def set_normed(values, scale):
        normed = values.astype(F32) * scale
        nrm[...] = normed.astype(BF16)
        nrm_t[...] = jnp.transpose(normed).astype(BF16)

    @pl.when(sec == 0)
    def _():
        load_h.wait()
        entered = h0[...].astype(F32)
        early_z(row_sums(entered * entered))
        load_w.wait()
        scatter_first(h0, 0, 4)
        load_c.wait()
        early_y()
        scatter_rest(zra, za_r, True, early_x)
        scale = scale_of(early_total())
        set_normed(h0[...], scale)
        gather_rest(True)
        normed = nrm[...].astype(F32)
        gu[...] = gf[0, 0, 0, high]
        arrived(ad, ex_r.at[0])
        scatter_sent(True)
        rest_sent()
        each(0, 16, lambda step: arrived(stats.at[1, (dp + 16 - step) % 16], st_r.at[1, step]))
        dot = columns(jnp.sum(stats[1], axis=0))[:, 0:1]
        own[...] = (
            gf[0, 0, 0].astype(F32) + scale * (back[...] - normed * dot / width)
        ).astype(BF16)
        send(own.at[high], gu, ex_s.at[0], ex_r.at[1], 1, dp)
        gd[...] = own[low]
        arrived(au, ex_r.at[2])
        sent(own.at[high], ex_s.at[0])

    @pl.when(sec == 1)
    def _():
        load_c.wait()
        gather_own(cot, 1, False)
        gf[0, 0, 0] = cot[...]
        load_h.wait()
        entered = h0[...].astype(F32)
        early_z(row_sums(entered * entered))
        load_w.wait()
        gather_rest(False, early_y, early_x)
        scale = scale_of(early_total())
        each(0, 4, lambda dz: arrived(zra.at[dz], za_r.at[dz]))
        mixed = (
            zra[0].astype(F32) + zra[1].astype(F32) + zra[2].astype(F32) + zra[3].astype(F32)
        )
        grown[...] = scale * mixed
        hid[...] = (h0[...].astype(F32) + grown[...]).astype(BF16)
        hidden = hid[...].astype(F32)
        first = lax.broadcasted_iota(jnp.int32, (8, tok), 0) == 0
        stat_send(0, jnp.where(first, row_sums(hidden * hidden), row_sums(back[...] * hidden)))
        scatter_first(hid, 0, 4)
        own_sent(cot, False)
        totals = stat_total(0)
        scale = scale_of(totals)
        dot = totals[:, 1:2] * scale
        nrm[...] = (hid[...].astype(F32) * scale).astype(BF16)
        own[...] = (
            cot[...].astype(F32) + scale * (back[...] - nrm[...].astype(F32) * dot / width)
        ).astype(BF16)
        gather_own(own, 0, True)
        early[0] = row_sums(own[...].astype(F32) * grown[...])[0:2]
        each(0, 16, lambda step: send(
            early.at[0], stats.at[1, dp], st_s.at[1, step], st_r.at[1, step], 0, (dp + step) % 16))
        nrm_t[...] = jnp.transpose(nrm[...].astype(F32)).astype(BF16)
        send(hid.at[low], ad, ex_s.at[0], ex_r.at[0], 0, dp)
        au[...] = hid[high]
        gd[...] = own[low]
        rest_sent()
        scatter_rest(zrb, zb_r, False)
        mixed = tz[0].astype(F32)
        for dz in (1, 2, 3):
            arrived(zrb.at[dz], zb_r.at[dz])
            mixed = mixed + zrb[dz].astype(F32)
        tz[0] = (hid[...].astype(F32) + scale * mixed).astype(BF16)
        send(tz.at[0, high], au, ex_s.at[1], ex_r.at[2], 0, dp)
        ad[...] = tz[0, low]
        own_sent(own, True)
        scatter_sent(False)
        stat_sent(0)
        each(0, 16, lambda step: sent(early.at[0], st_s.at[1, step]))
        sent(hid.at[low], ex_s.at[0])
        sent(tz.at[0, high], ex_s.at[1])
        arrived(gu, ex_r.at[1])


def finish_kernel(nrm_hbm, gf_hbm, *refs):
    held, outs = refs[:4], refs[4:8]
    wg_hbm, nrm_t, gf, wg, small, in_sem, wg_sem, held_sem, out_sem = refs[8:]
    cols = nrm_t.shape[0]
    dp = lax.axis_index("dp")

    def load(k):
        return pltpu.make_async_copy(gf_hbm.at[k // 4, (k // 2) % 2, k % 2], gf.at[k], in_sem.at[k])

    def write(k):
        spot = peer_block(dp, k // 4, (k // 2) % 2, k % 2) * cols
        return pltpu.make_async_copy(
            wg.at[k], wg_hbm.at[:, pl.ds(pl.multiple_of(spot, cols), cols)], wg_sem.at[k])

    load_n = pltpu.make_async_copy(nrm_hbm, nrm_t, held_sem.at[4])
    load_n.start()
    each(0, 16, lambda k: load(k).start())
    takes = [pltpu.make_async_copy(held[k], small.at[k], held_sem.at[k]) for k in range(4)]
    copies = [pltpu.make_async_copy(small.at[k], outs[k], out_sem.at[k]) for k in range(4)]
    for copy in takes:
        copy.start()
    load_n.wait()

    def step(k):
        load(k).wait()
        wg[k] = jnp.dot(nrm_t[...], gf[k], preferred_element_type=F32)
        write(k).start()

    each(0, 16, step)
    for take, copy in zip(takes, copies):
        take.wait()
        copy.start()
    for copy in copies:
        copy.wait()
    each(0, 16, lambda k: write(k).wait())


def direct_body(entering, cotangent, weights):
    streams, micro, tok_mb, cols = entering.shape
    tok = streams * micro * tok_mb
    half = tok // 2
    width = weights.shape[2]
    rows = entering.reshape(tok, cols)
    slopes = cotangent.reshape(tok, cols)
    vm = pl.BlockSpec(memory_space=pltpu.VMEM)
    hbm = pl.BlockSpec(memory_space=pl.ANY)
    half_out = jax.ShapeDtypeStruct((half, cols), BF16)
    dma = pltpu.SemaphoreType.DMA
    *kept, nrm_t, gathered = pl.pallas_call(
        window_kernel,
        out_shape=(half_out,) * 4 + (
            jax.ShapeDtypeStruct((cols, tok), BF16),
            jax.ShapeDtypeStruct((4, 2, 2, tok, cols), BF16),
        ),
        in_specs=[hbm, hbm, hbm],
        out_specs=(vm,) * 5 + (hbm,),
        scratch_shapes=[
            pltpu.VMEM((tok, cols), BF16),
            pltpu.VMEM((tok, cols), BF16),
            pltpu.VMEM((cols, width), BF16),
            pltpu.VMEM((4, 2, 2, tok, cols), BF16),
            pltpu.VMEM((4, 2, 2, tok, cols), BF16),
            pltpu.VMEM((4, 2, half, cols), BF16),
            pltpu.VMEM((4, 2, half, cols), BF16),
            pltpu.VMEM((4, half, cols), BF16),
            pltpu.VMEM((4, half, cols), BF16),
            pltpu.VMEM((4, half, cols), BF16),
            pltpu.VMEM((4, half, cols), BF16),
            pltpu.VMEM((4, tok, cols), BF16),
            pltpu.VMEM((4, tok, cols), BF16),
            pltpu.VMEM((4, tok, cols), BF16),
            pltpu.VMEM((2, 16, 2, tok), F32),
            pltpu.VMEM((tok, cols), F32),
            pltpu.VMEM((tok, cols), BF16),
            pltpu.VMEM((tok, cols), BF16),
            pltpu.VMEM((tok, cols), BF16),
            pltpu.VMEM((tok, cols), F32),
            pltpu.VMEM((8, 2, tok), F32), dma((6,)), dma((6,)),
            dma((3,)), dma((16,)), dma((2, 16)), dma((2, 16)),
            dma((4, 4)), dma((4, 5)), dma((6,)),
            dma((4, 4)), dma((4, 4)), dma((4,)), dma((4,)), dma((4,)),
            dma((2,)), dma((3,)),
        ],
        compiler_params=pltpu.CompilerParams(
            collective_id=0, has_side_effects=True, vmem_limit_bytes=63 * 1024 * 1024
        ),
        cost_estimate=pl.CostEstimate(
            flops=4 * tok * cols * width, bytes_accessed=4 * cols * width, transcendentals=2 * tok
        ),
    )(rows, slopes, weights)
    *outs, weight_grad = pl.pallas_call(
        finish_kernel,
        out_shape=(half_out,) * 4 + (jax.ShapeDtypeStruct((cols, width), F32),),
        in_specs=[hbm] * 6,
        out_specs=(hbm,) * 5,
        scratch_shapes=[
            pltpu.VMEM((cols, tok), BF16),
            pltpu.VMEM((16, tok, cols), BF16),
            pltpu.VMEM((16, cols, cols), F32),
            pltpu.VMEM((4, half, cols), BF16),
            dma((16,)), dma((16,)), dma((5,)), dma((4,)),
        ],
        compiler_params=pltpu.CompilerParams(vmem_limit_bytes=63 * 1024 * 1024),
        cost_estimate=pl.CostEstimate(
            flops=2 * tok * cols * width, bytes_accessed=6 * cols * width, transcendentals=0
        ),
    )(nrm_t, gathered, *kept)
    shape = (1, micro, tok_mb, cols)
    return (*(out.reshape(shape) for out in outs), weight_grad[None])


def solution(mesh):
    placed = (P(None, None, None, "dp"), P(None, None, None, "dp"), P("section", "dp", None))
    exact = dict(mesh.shape) == {"section": 2, "dp": 16}
    return jax.shard_map(
        direct_body if exact else body,
        mesh=mesh,
        in_specs=placed,
        out_specs=(
            P("section", None, None, "dp"),
            P("section", None, None, "dp"),
            P("section", None, None, "dp"),
            P("section", None, None, "dp"),
            P("section", "dp", None),
        ),
        check_vma=False,
    )
```
